256 devices in a mesh: row: 16 (over x, y), col: 16 (over z, core).
Axes of the slice: x: 4, y: 4, z: 8, core: 2. Of those that a mesh axis runs over, the one named last changes fastest.
Arguments:
- iterate: float32 [6, 24576, 320], P(None, ('row', 'col')), may hold values from -6 to 6
- residual: float32 [6, 24576, 320], P(None, ('row', 'col')), may hold values from -114 to 114
- shadow: float32 [2, 24576, 320], P(None, ('row', 'col')), may hold values from -6 to 6
- res_dirs: float32 [2, 6, 24576, 320], P(None, None, ('row', 'col')), may hold values from -75 to 75
- sol_dirs: float32 [2, 6, 24576, 320], P(None, None, ('row', 'col')), may hold values from -69 to 69
- omega_step: float32 [6], replicated, may hold values from 0.3 to 1
- face_blocks: bfloat16 [24576, 4, 80, 80], P(('row', 'col')), may hold values from -1 to 1
- send_list: int32 [1024, 48], P(('row', 'col')), may hold values from 0 to 95
- neighbour_perm: int32 [256, 384], P(('row', 'col')), may hold values from 0 to 383, each once within a row
- wall_perm: int32 [256, 96], P(('row', 'col')), may hold values from 0 to 95, each once within a row
- wall_count: int32 [256], P(('row', 'col')), may hold values from 1 to 48, 6144 in all
- wall_coef: bfloat16 [3, 5, 196608], P(None, None, ('row', 'col')), may hold values from -2.5 to 2.5
- rbf_support: int32 [1536, 4], P(('row', 'col')), may hold values from 0 to 95
- rbf_weights: bfloat16 [1536, 4, 128, 128], P(('row', 'col')), may hold values from -0.25 to 0.25
Outputs:
- iterate_out: float32 [6, 24576, 320], P(None, ('row', 'col'))
- residual_out: float32 [6, 24576, 320], P(None, ('row', 'col'))
- smoothed: float32 [18, 196608], P(None, ('row', 'col'))
The draws below stay inside these ranges and needn't reach their ends.
Inputs may be any that keep to these rules, and one draw needn't show every extreme that they name: `neighbour_perm`: each device's row lists every one of its 384 face slots once. `wall_perm`: each device's row lists every local element once. `wall_count`: some device has exactly 48 wall elements.
All inputs are finite; a program needn't handle non-finite values.
Results may differ from the reference program's by a relative error of at most 0.0065.
Values may be sent and summed in bfloat16 or wider, within the bound.
No kernel may reach another device: no remote copies, remote signals or barrier semaphores. Data moves between devices by JAX's collectives and lax.ppermute only.
A program may use at most 128 MiB of HBM per device.

```python
import math
import jax
import jax.numpy as jnp
import numpy as np
from jax import lax

NVAR = 5
NODES1D = 4
NOBJ = 6
E = 96
NSUP = 4
PB = 128
H = 48
WMAX = 48
BLOCK = 320
TRACE = 80
NBLK = 6
NELEM = 24576
NPTS = 196608
N_ROW = 16
N_COL = 16


def shadow_field(key):
    shadow_key = jax.random.fold_in(key, 101)
    var_index = jnp.arange(BLOCK, dtype=jnp.int32) // NODES1D ** 3
    owner = (var_index[None, :] % 2 == jnp.arange(2, dtype=jnp.int32)[:, None]).astype(jnp.float32)
    amounts = jax.random.uniform(jax.random.fold_in(key, 102), (2, NVAR), jnp.float32, 1.2, 1.5)
    sign_bits = jax.random.randint(jax.random.fold_in(key, 103), (2, NVAR), 0, 2)
    signs = (2 * sign_bits - 1).astype(jnp.float32)
    per_variable = amounts * signs
    common = jnp.take(per_variable, var_index, axis=1) * owner
    values = jax.random.truncated_normal(shadow_key, -4.0, 4.0, (2, NELEM, BLOCK), jnp.float32)
    return values + common[:, None, :]


def noise_field(key, label, shape):
    noise_key = jax.random.fold_in(key, label)
    values = jax.random.truncated_normal(noise_key, -6.0, 6.0, shape, jnp.float32)
    return values


def position_rise():
    return 1.0 + 2.0 * jnp.arange(NELEM, dtype=jnp.float32)[:, None] / NELEM


def draw_shadow(key, part):
    return shadow_field(key)


def draw_res_dirs(key, part):
    shadow = shadow_field(key)
    gains = jax.random.uniform(jax.random.fold_in(key, 201), (2, NOBJ, 1, 1), jnp.float32, 1.5, 2.5)
    return gains * shadow[:, None] + noise_field(key, 202, (2, NOBJ, NELEM, BLOCK))


def draw_sol_dirs(key, part):
    shadow = shadow_field(key)
    gains = jax.random.uniform(jax.random.fold_in(key, 203), (2, NOBJ, 1, 1), jnp.float32, 0.2, 0.5)
    return -gains * position_rise() * shadow[:, None] + noise_field(key, 204, (2, NOBJ, NELEM, BLOCK))


def draw_residual(key, part):
    shadow = shadow_field(key)
    gains = jax.random.uniform(jax.random.fold_in(key, 205), (2, NOBJ, 1, 1), jnp.float32, 0.5, 1.5)
    aligned = jnp.sum(gains * shadow[:, None], axis=0) * position_rise()
    return aligned + noise_field(key, 206, (NOBJ, NELEM, BLOCK))


def draw_face_blocks(key, part):
    noise_key = jax.random.fold_in(key, 301)
    spread = (2.0 * TRACE) ** (-0.5)
    noise = jax.random.truncated_normal(noise_key, -2.5, 2.5, (NELEM, 4, TRACE, TRACE), jnp.float32)
    bias = jax.random.uniform(jax.random.fold_in(key, 302), (NELEM, 4, 1, 1), jnp.float32, 0.15, 0.3)
    diagonal = jnp.eye(TRACE, dtype=jnp.float32)[None, None]
    return (noise * spread + bias * diagonal).astype(jnp.bfloat16)


def touch_ends(entries, rng, least, largest):
    index_at = [jax.random.randint(jax.random.fold_in(rng, axis), (), 0, length) for axis, length in enumerate(entries.shape)]
    longest = entries.shape.index(max(entries.shape))
    beside = index_at[:longest] + [(index_at[longest] + 1) % entries.shape[longest]] + index_at[longest + 1:]
    return entries.at[tuple(index_at)].set(least).at[tuple(beside)].set(largest)


def levels(key, shape, split, low, high):
    gain, own = 1.0, jax.random.fold_in(key, 6)
    for dim, blocks in split:
        steps = jnp.exp(jax.random.uniform(jax.random.fold_in(own, dim), (blocks,), jnp.float32, low / len(split), high / len(split)))
        gain = gain * jnp.repeat(steps, shape[dim] // blocks).reshape([-1 if axis == dim else 1 for axis in range(len(shape))])
    return gain


def length_profile(amount, total, bound, slope):
    portions = [(1 << 20) // math.isqrt(standing ** slope) + 1 for standing in range(2, amount + 1)]
    rest, given = total - bound - (amount - 1), [1] * (amount - 1)
    while rest > 0:
        candidates = [i for i in range(amount - 1) if given[i] < bound]
        whole, remaining = sum([portions[i] for i in candidates]), rest
        for i in candidates:
            extra = min(bound - given[i], max(1, remaining * portions[i] // whole), rest)
            given[i] = given[i] + extra
            rest = rest - extra
    return np.array([bound] + given)


def ragged(stream_key, amount, total, limit, skew):
    if amount == 2:
        one = jax.random.randint(stream_key, (), max(1, total - limit), min(limit, total - 1) + 1)
        return jnp.stack([one, total - one])
    tallies = jnp.asarray(length_profile(amount, total, limit, skew), jnp.int32)
    twos = (amount - 1) // 2
    donor, sink = tallies[1:1 + 2 * twos:2], tallies[2:2 + 2 * twos:2]
    margin = jnp.minimum(donor - 1, limit - sink)
    shifted = jax.random.randint(jax.random.fold_in(stream_key, 1), (twos,), 0, 1 << 20) % (margin + 1)
    tallies = tallies.at[1:1 + 2 * twos:2].set(donor - shifted).at[2:2 + 2 * twos:2].set(sink + shifted)
    return tallies[jax.random.permutation(jax.random.fold_in(stream_key, 2), amount)]


def gaussian(stream_key, shape, scale, most, pieces=(), kind=jnp.bfloat16):
    array = jax.random.normal(stream_key, shape, jnp.float32) * scale
    if len(pieces) > 0:
        array = levels(stream_key, shape, pieces, -0.22, 0.18) * array
    return jnp.clip(array, min=-most, max=most).astype(kind)


def setup_inputs(seed: int = 0) -> dict:
    streams_of = jax.random.split(jax.random.key(seed), 15)
    return {
        "iterate": gaussian(streams_of[0], (NOBJ, NELEM, BLOCK), 1.0, 6.0, ((1, 256),), jnp.float32),
        "residual": draw_residual(jax.random.fold_in(streams_of[14], 71), 0),
        "shadow": draw_shadow(jax.random.fold_in(streams_of[14], 71), 0),
        "res_dirs": draw_res_dirs(jax.random.fold_in(streams_of[14], 71), 0),
        "sol_dirs": draw_sol_dirs(jax.random.fold_in(streams_of[14], 71), 0),
        "omega_step": jnp.clip(jnp.exp(jax.random.uniform(streams_of[5], (NOBJ,), jnp.float32, math.log(0.3), math.log(1.0))), 0.3, 1.0),
        "face_blocks": draw_face_blocks(jax.random.fold_in(streams_of[14], 71), 0),
        "send_list": touch_ends(jax.random.randint(streams_of[7], (4 * N_ROW * N_COL, H), 0, E), jax.random.fold_in(streams_of[7], 1), 0, E - 1).astype(jnp.int32),
        "neighbour_perm": jax.vmap(lambda own: jax.random.permutation(own, 4 * E))(jax.random.split(streams_of[8], (N_ROW * N_COL))).reshape((N_ROW * N_COL, 4 * E)).astype(jnp.int32),
        "wall_perm": jax.vmap(lambda own: jax.random.permutation(own, E))(jax.random.split(streams_of[9], (N_ROW * N_COL))).reshape((N_ROW * N_COL, E)).astype(jnp.int32),
        "wall_count": ragged(streams_of[10], N_ROW * N_COL, N_ROW * N_COL * WMAX // 2, WMAX, 2).astype(jnp.int32),
        "wall_coef": gaussian(streams_of[11], (3, NVAR, NPTS), NVAR ** -0.5, 2.5, ((2, 256),)),
        "rbf_support": touch_ends(jax.random.randint(streams_of[12], (N_ROW * N_COL * NBLK, NSUP), 0, N_ROW * NBLK), jax.random.fold_in(streams_of[12], 1), 0, (N_ROW * NBLK) - 1).astype(jnp.int32),
        "rbf_weights": gaussian(streams_of[13], (N_ROW * N_COL * NBLK, NSUP, PB, PB), (NSUP * PB) ** -0.5, 0.25, ((0, 256),)),
    }


top_precision = lax.Precision.HIGHEST


def face_traces(vectors):
    batch_size, elem_count = vectors.shape[0], vectors.shape[1]
    nodes_view = vectors.reshape(batch_size, elem_count, NVAR, NODES1D, NODES1D, NODES1D)
    outer_node = NODES1D - 1
    stacked = jnp.stack([nodes_view[:, :, :, outer_node], nodes_view[:, :, :, 0],
                         nodes_view[:, :, :, :, outer_node], nodes_view[:, :, :, :, 0]], axis=2)
    return stacked.reshape(batch_size, elem_count, 4, TRACE)


def lift_faces(vectors, coupled):
    batch_size, elem_count = vectors.shape[0], vectors.shape[1]
    nodes_view = vectors.reshape(batch_size, elem_count, NVAR, NODES1D, NODES1D, NODES1D)
    pieces_view = coupled.reshape(batch_size, elem_count, 4, NVAR, NODES1D, NODES1D)
    outer_node = NODES1D - 1
    nodes_view = nodes_view.at[:, :, :, outer_node].add(pieces_view[:, :, 0])
    nodes_view = nodes_view.at[:, :, :, 0].add(pieces_view[:, :, 1])
    nodes_view = nodes_view.at[:, :, :, :, outer_node].add(pieces_view[:, :, 2])
    nodes_view = nodes_view.at[:, :, :, :, 0].add(pieces_view[:, :, 3])
    return nodes_view.reshape(batch_size, elem_count, BLOCK)


def apply_global(vectors, face_blocks, send_list, neighbour_perm):
    batch_size = vectors.shape[0]
    local_traces = face_traces(vectors).reshape(batch_size, N_ROW, N_COL, E, 4, TRACE)
    send_rows = send_list.reshape(N_ROW, N_COL, 4, H).astype(jnp.int32)
    outgoing = []
    for direction in range(4):
        index_map = send_rows[None, :, :, direction, :, None]
        outgoing.append(jnp.take_along_axis(local_traces[:, :, :, :, direction], index_map, axis=3))
    row_pad = jnp.zeros((batch_size, 1, N_COL, H, TRACE), jnp.float32)
    col_pad = jnp.zeros((batch_size, N_ROW, 1, H, TRACE), jnp.float32)
    from_lower = jnp.concatenate([row_pad, outgoing[0][:, :-1]], axis=1)
    from_upper = jnp.concatenate([outgoing[1][:, 1:], row_pad], axis=1)
    from_left = jnp.concatenate([col_pad, outgoing[2][:, :, :-1]], axis=2)
    from_right = jnp.concatenate([outgoing[3][:, :, 1:], col_pad], axis=2)
    received = jnp.stack([from_lower, from_upper, from_left, from_right], axis=3)
    received = received.reshape(batch_size, N_ROW, N_COL, 4 * H, TRACE)
    table = jnp.concatenate([received, local_traces.reshape(batch_size, N_ROW, N_COL, 4 * E, TRACE)], axis=3)
    slot_number = neighbour_perm.reshape(N_ROW, N_COL, 4 * E).astype(jnp.int32)
    table_index = jnp.where(slot_number < 4 * H, slot_number, slot_number + 4 * H)
    read_traces = jnp.take_along_axis(table, table_index[None, :, :, :, None], axis=3)
    read_rows = jnp.moveaxis(read_traces.reshape(batch_size, N_ROW, N_COL, E, 4, TRACE), 1, 0)
    block_rows = face_blocks.reshape(N_ROW, N_COL, E, 4, TRACE, TRACE)

    def couple_row(pair):
        return jnp.einsum("vcefi,cefij->vcefj", pair[0], pair[1].astype(jnp.float32), precision=top_precision)

    coupled = jnp.moveaxis(lax.map(couple_row, (read_rows, block_rows)), 0, 1)
    return lift_faces(vectors, coupled.reshape(batch_size, NELEM, 4 * TRACE))


def project(shadow, vectors):
    return jnp.einsum("ieb,keb->ki", shadow, vectors, precision=top_precision)


def solve_pair(matrix, rhs):
    determinant = matrix[:, 0, 0] * matrix[:, 1, 1] - matrix[:, 0, 1] * matrix[:, 1, 0]
    first_coeff = (matrix[:, 1, 1] * rhs[:, 0] - matrix[:, 0, 1] * rhs[:, 1]) / determinant
    second_coeff = (matrix[:, 0, 0] * rhs[:, 1] - matrix[:, 1, 0] * rhs[:, 0]) / determinant
    return jnp.stack([first_coeff, second_coeff], axis=1)


def combine_pair(first_vec, second_vec, coeffs):
    return first_vec * coeffs[:, 0, None, None] + second_vec * coeffs[:, 1, None, None]


def wall_sensitivity(iterate_out, wall_coef, wall_perm, wall_count):
    device_count = N_ROW * N_COL
    node_area = NODES1D * NODES1D
    nodes_view = iterate_out.reshape(NOBJ, device_count, E, NVAR, NODES1D, NODES1D, NODES1D)[..., 0]
    wall_layer = nodes_view.reshape(NOBJ, device_count, E, NVAR, node_area)
    chosen = wall_perm[:, :WMAX].astype(jnp.int32)
    picked = jnp.take_along_axis(wall_layer, chosen[None, :, :, None, None], axis=2)
    live_slots = (jnp.arange(WMAX)[None, :] < wall_count[:, None]).astype(jnp.float32)
    coef_view = wall_coef.reshape(3, NVAR, device_count, WMAX, node_area).astype(jnp.float32)
    sens = jnp.einsum("dvnwp,knwvp->dknwp", coef_view, picked, precision=top_precision)
    sens = sens * live_slots[None, None, :, :, None]
    return sens.reshape(3 * NOBJ, NPTS).astype(jnp.bfloat16)


def smooth_global(sens, rbf_support, rbf_weights):
    comp_count = sens.shape[0]
    grouped = sens.reshape(comp_count, N_ROW, N_COL, NBLK, PB)
    support = rbf_support.reshape(N_ROW, N_COL, NBLK, NSUP).astype(jnp.int32)
    source_row = support // NBLK
    source_block = support % NBLK
    column_index = jnp.arange(N_COL).astype(jnp.int32)[None, :, None, None]
    picked = grouped[:, source_row, column_index, source_block, :]
    weights = rbf_weights.reshape(N_ROW, N_COL, NBLK, NSUP, PB, PB).astype(jnp.float32)
    smoothed = jnp.einsum("crbljq,rbljqp->crblp", picked.astype(jnp.float32), weights, precision=top_precision)
    return smoothed.reshape(comp_count, NPTS)


def reference(iterate, residual, shadow, res_dirs, sol_dirs, omega_step, face_blocks, send_list,
              neighbour_perm, wall_perm, wall_count, wall_coef, rbf_support, rbf_weights):
    weight = omega_step[:, None, None]

    def operator(vectors):
        return apply_global(vectors, face_blocks, send_list, neighbour_perm)

    first_rhs = project(shadow, residual)
    matrix_now = jnp.einsum("ieb,jkeb->kij", shadow, res_dirs, precision=top_precision)
    coeff_one = solve_pair(matrix_now, first_rhs)
    vec_one = residual - combine_pair(res_dirs[0], res_dirs[1], coeff_one)
    step_one = weight * vec_one - combine_pair(sol_dirs[0], sol_dirs[1], coeff_one)
    change_one = -operator(step_one)
    resid_one = residual + change_one
    iter_one = iterate + step_one
    new_column = project(shadow, change_one)
    matrix_next = matrix_now.at[:, :, 0].set(new_column)
    second_rhs = project(shadow, resid_one)
    coeff_two = solve_pair(matrix_next, second_rhs)
    vec_two = resid_one - combine_pair(change_one, res_dirs[1], coeff_two)
    step_two = weight * vec_two - combine_pair(step_one, sol_dirs[1], coeff_two)
    change_two = -operator(step_two)
    residual_out = resid_one + change_two
    iterate_out = iter_one + step_two
    sens = wall_sensitivity(iterate_out, wall_coef, wall_perm, wall_count)
    smoothed = smooth_global(sens, rbf_support, rbf_weights)
    return (iterate_out, residual_out, smoothed)
```

```python
import functools

import jax
import jax.numpy as jnp
import numpy as np
from jax import lax
from jax.experimental import pallas as pl
from jax.experimental.pallas import tpu as pltpu
from jax.sharding import PartitionSpec as P

NVAR = 5
NOBJ = 6
E = 96
H = 48
WMAX = 48
BLOCK = 320
TRACE = 80
LANES = 128
NBLK = 6
NSUP = 4
NBAS = 3
NVEC = NOBJ * NBAS
WIDE = NVEC * LANES
STEP = NBAS * LANES
SLOTS = 4 * H
FACES = 4 * E
VPAD = 24
BPAD = 24
F32 = jnp.float32
BF16 = jnp.bfloat16


def selection():
    sel = np.zeros((BLOCK, 4 * LANES), np.float32)
    for var in range(NVAR):
        for a in range(4):
            for c in range(4):
                i = var * 16 + a * 4 + c
                base = var * 64
                sel[base + 48 + a * 4 + c, 0 * LANES + i] = 1
                sel[base + a * 4 + c, 1 * LANES + i] = 1
                sel[base + a * 16 + 12 + c, 2 * LANES + i] = 1
                sel[base + a * 16 + c, 3 * LANES + i] = 1
    return sel


def wall_spread():
    out = np.zeros((BLOCK, LANES), np.float32)
    for var in range(NVAR):
        for p in range(16):
            out[var * 64 + p * 4, p::16] = 1
    return out


def dot(a, b, dims=((1,), (0,))):
    return lax.dot_general(a, b, (dims, ((), ())), preferred_element_type=F32)


def split(x):
    high = x.astype(BF16)
    return high, (x - high.astype(F32)).astype(BF16)


def one_hot_rows(index, width):
    lane = lax.broadcasted_iota(jnp.int32, (index.shape[0], width), 1)
    return jnp.where(lane == index, 1.0, 0.0).astype(BF16)


def picker(send_row):
    row = lax.broadcasted_iota(jnp.int32, (E, H), 0)
    return jnp.where(row == send_row, 1.0, 0.0).astype(BF16)


def basis_kernel(om, send, sel, r, d, s, sh, dots, thi, tlo, outgo):
    k = pl.program_id(0)
    w = om[k]
    r0, d0, d1 = r[0], d[0, 0], d[1, 0]
    us = [w * r0, w * d0 + s[0, 0], w * d1 + s[1, 0]]
    for x, vec in enumerate([r0, d0, d1] + us):
        for i in range(2):
            dots[0, pl.ds(2 * x + i, 1), :] = jnp.sum(sh[i] * vec, axis=0, keepdims=True)
    dots[0, 12:16, :] = jnp.zeros((4, BLOCK), F32)
    picks = [picker(send[f : f + 1, :]) for f in range(4)]
    for m, u in enumerate(us):
        at = slice(m * LANES, (m + 1) * LANES)
        high, low = split(u)
        traces = dot(high, sel[...]).astype(BF16)
        rest = dot(low[H:], sel[...]).astype(BF16)
        for f in range(4):
            face = traces[:, f * LANES : (f + 1) * LANES]
            thi[f * H : (f + 1) * H, at] = face[H:]
            tlo[f * H : (f + 1) * H, at] = rest[:, f * LANES : (f + 1) * LANES]
            outgo[f, :, at] = dot(picks[f], face, ((0,), (0,))).astype(BF16)


def blocks_kernel(_, b, sh, selt, eye, wt, q, scratch, qscr):
    trsh = []
    for i in range(2):
        high, low = split(sh[i])
        nt = ((1,), (1,))
        trsh.append((dot(selt[...], high, nt) + dot(selt[...], low, nt))[:TRACE])

    def step(n, carry):
        for c in range(8):
            i = n * 8 + c
            x = b[0, i]
            scratch[pl.ds(i, E, stride=TRACE), 0:TRACE] = dot(eye[...], x, ((1,), (1,)))
            x = x.astype(F32)
            for a in range(2):
                qscr[a, pl.ds(i, 1), :] = jnp.sum(x * trsh[a], axis=0, keepdims=True)
        return carry

    lax.fori_loop(0, TRACE // 8, step, 0)

    def pack(n, carry):
        for c in range(4):
            e = n * 4 + c
            at = pl.ds(pl.multiple_of(e * TRACE, TRACE), TRACE)
            wt[0, e] = scratch[at, 0:TRACE].astype(BF16)
        return carry

    lax.fori_loop(0, E // 4, pack, 0)
    for a in range(2):
        q[a, :, 0:TRACE] = qscr[a].T
        q[a, :, TRACE:LANES] = jnp.zeros((E, LANES - TRACE), F32)


def received(flags, recv, at):
    return [jnp.where(flags[d] > 0, ref[:, at], jnp.zeros((), BF16)) for d, ref in enumerate(recv)]


def reduce_kernel(flags, cidx, thi, tlo, r0, r1, r2, r3, q, dots, out, hot, rows, acc):
    k = pl.program_id(0)

    @pl.when(k == 0)
    def _():
        hot[...] = one_hot_rows(cidx[...], 2 * SLOTS)
        rows[...] = jnp.zeros_like(rows)
        acc[...] = jnp.zeros_like(acc)

    full = slice(0, STEP)
    table = jnp.concatenate(received(flags, (r0, r1, r2, r3), full) + [thi[...]], axis=0)
    t = dot(hot[...], table) + dot(hot[:, SLOTS:], tlo[...])
    for m in range(NBAS):
        for i in range(2):
            part = t[:, m * LANES : (m + 1) * LANES] * q[i]
            rows[pl.ds(6 + 2 * m + i, 1), :] = jnp.sum(part, axis=0, keepdims=True)
    col = jnp.sum(rows[...], axis=1, keepdims=True) + jnp.sum(dots[0], axis=1, keepdims=True)
    lane = lax.broadcasted_iota(jnp.int32, (16, LANES), 1)
    acc[...] += jnp.where(lane == k, col, 0.0)
    out[...] = jnp.broadcast_to(acc[...][None], out.shape)


def merge_kernel(x, out):
    out[...] = jnp.broadcast_to(jnp.sum(x[...], axis=0, keepdims=True), out.shape)


def couple(t_ref, wt, y_ref, pad):
    def step(n, carry):
        for c in range(8):
            face = n * 8 + c
            at = pl.ds(pl.multiple_of(face * pad, 8), pad)
            y_ref[at, 0:TRACE] = dot(t_ref[at, 0:TRACE].astype(BF16), wt[face])
        return carry

    lax.fori_loop(0, FACES // 8, step, 0)


def apply_kernel(flags, cidx, send, thi, tlo, r0, r1, r2, r3, wt, cross, _, outgo, yn, t_ref, y_ref):
    hot = one_hot_rows(cidx[...], 2 * SLOTS)
    for k in range(NOBJ):
        at = slice(k * STEP, (k + 1) * STEP)
        table = jnp.concatenate(received(flags, (r0, r1, r2, r3), at) + [thi[:, at]], axis=0)
        t = dot(hot, table)
        for f in range(4):
            for m in range(NBAS):
                rows = pl.ds(f * E * VPAD + k * NBAS + m, E, stride=VPAD)
                t_ref[rows, :] = t[f * E : (f + 1) * E, m * LANES : (m + 1) * LANES]
    couple(t_ref, wt, y_ref, VPAD)
    picks = [picker(send[f : f + 1, :]) for f in range(4)]
    for v in range(NVEC):
        total = None
        for f in range(4):
            y = y_ref[pl.ds(f * E * VPAD + v, E, stride=VPAD), :][:, 0:TRACE]
            yn[v, f, :, 0:TRACE] = y
            part = dot(y.astype(BF16), cross[f * LANES : f * LANES + TRACE, :])
            total = part if total is None else total + part
        total = total.astype(BF16)
        for f in range(4):
            face = total[:, f * LANES : (f + 1) * LANES]
            outgo[f, :, v * LANES : (v + 1) * LANES] = dot(picks[f], face, ((0,), (0,))).astype(BF16)


def solve(m00, m01, m10, m11, f0, f1):
    det = m00 * m11 - m01 * m10
    return (m11 * f0 - m01 * f1) / det, (m00 * f1 - m10 * f0) / det


def step_kernel(
    red, om, r, d, s, it, yn, selt, wsel, coef, spread, itout, base, st2, coefs, payload, co, scr
):
    k = pl.program_id(0)

    @pl.when(k == 0)
    def _():
        t = jnp.sum(red[...], axis=0)
        row = lambda n: t[n : n + 1]
        w = om[...]
        c0, c1 = solve(row(2), row(4), row(3), row(5), row(0), row(1))
        n0 = -(row(6) - c0 * row(8) - c1 * row(10))
        n1 = -(row(7) - c0 * row(9) - c1 * row(11))
        e0, e1 = solve(n0, row(4), n1, row(5), row(0) + n0, row(1) + n1)
        gamma = w * (1.0 - e0)
        delta = gamma + e0
        for n, x in enumerate([w, c0, c1, 1.0 - delta, delta * c0, delta * c1 - e1, gamma]):
            co[pl.ds(n, 1), :] = x
        co[7:8, :] = jnp.zeros((1, LANES), F32)
        coefs[...] = co[...]
        scr[...] = jnp.zeros_like(scr)

    lane = lax.broadcasted_iota(jnp.int32, (8, LANES), 1)
    col = jnp.sum(jnp.where(lane == k, co[...], 0.0), axis=1, keepdims=True)
    c = [col[n : n + 1] for n in range(7)]
    r0 = r[0]
    u0 = c[0] * r0
    u1 = c[0] * d[0, 0] + s[0, 0]
    u2 = c[0] * d[1, 0] + s[1, 0]
    st1 = u0 - c[1] * u1 - c[2] * u2
    lift = None
    for f in range(4):
        y = yn[0, f] - c[1] * yn[1, f] - c[2] * yn[2, f]
        high, low = split(y[:, 0:TRACE])
        block = selt[f * LANES : f * LANES + TRACE, :]
        part = dot(high, block) + dot(low, block)
        lift = part if lift is None else lift + part
    two = c[3] * u0 + c[4] * u1 + c[5] * u2 - c[6] * lift
    new = it[0] + st1 + two
    itout[0] = new
    st2[0] = two
    base[0] = r0 - st1 - lift - two
    high, low = split(new)
    picked = dot(wsel[...], high) + dot(wsel[...], low)
    slot = lax.broadcasted_iota(jnp.int32, (WMAX, LANES), 0) % 8
    group = lax.broadcasted_iota(jnp.int32, (WMAX, LANES), 1) // 16
    for a in range(3):
        high, low = split(picked * coef[a])
        part = dot(high, spread[...]) + dot(low, spread[...])
        part = jnp.where(slot == group, part, 0.0).reshape(NBLK, 8, LANES)
        scr[pl.ds(a * NOBJ + k, NBLK, stride=BPAD), :] = jnp.sum(part, axis=1)

    @pl.when(k == NOBJ - 1)
    def _():
        payload[...] = jnp.broadcast_to(scr[...].astype(BF16)[None], payload.shape)


def last_kernel(
    flags, coefs, cidx, st2, base, a0, a1, a2, a3, b0, b1, b2, b3, wt, sel, selt, _, out, t_ref, y_ref
):
    hot = one_hot_rows(cidx[...], 2 * SLOTS)
    for k in range(NOBJ):
        c = [coefs[n : n + 1, k : k + 1] for n in range(7)]
        rows = []
        for d, (a, b) in enumerate(zip((a0, a1, a2, a3), (b0, b1, b2, b3))):
            u = [a[:, (k * NBAS + m) * LANES : (k * NBAS + m + 1) * LANES].astype(F32) for m in range(3)]
            y = [b[:, (k * NBAS + m) * LANES : (k * NBAS + m + 1) * LANES].astype(F32) for m in range(3)]
            x = c[3] * u[0] + c[4] * u[1] + c[5] * u[2] - c[6] * (y[0] - c[1] * y[1] - c[2] * y[2])
            rows.append(jnp.where(flags[d] > 0, x, 0.0).astype(BF16))
        local = dot(st2[k, H:, :].astype(BF16), sel[...]).astype(BF16)
        rows += [local[:, f * LANES : (f + 1) * LANES] for f in range(4)]
        t = dot(hot, jnp.concatenate(rows, axis=0))
        for f in range(4):
            t_ref[pl.ds(f * E * 8 + k, E, stride=8), :] = t[f * E : (f + 1) * E]
    couple(t_ref, wt, y_ref, 8)
    for k in range(NOBJ):
        lift = None
        for f in range(4):
            high, low = split(y_ref[pl.ds(f * E * 8 + k, E, stride=8), :][:, 0:TRACE])
            block = selt[f * LANES : f * LANES + TRACE, :]
            part = dot(high, block) + dot(low, block)
            lift = part if lift is None else lift + part
        out[k] = base[k] - lift


def smooth_kernel(support, sens, weights, out, scr):
    scr[...] = sens[...].astype(F32)
    for m in range(NBLK):
        acc = None
        for s in range(NSUP):
            at = pl.multiple_of(support[m, s] * BPAD, 8)
            part = dot(scr[pl.ds(at, BPAD), :].astype(BF16), weights[m, s])
            acc = part if acc is None else acc + part
        out[:, m * LANES : (m + 1) * LANES] = acc[: 3 * NOBJ]


SMEM = pl.BlockSpec(memory_space=pltpu.SMEM)
ANY = pl.BlockSpec(memory_space=pl.ANY)
VMEM = pl.BlockSpec(memory_space=pltpu.VMEM)
call = functools.partial(pl.pallas_call)


def params(mib):
    return pltpu.CompilerParams(vmem_limit_bytes=mib << 20)


def cost(us):
    return pl.CostEstimate(flops=int(us * 5e8), bytes_accessed=int(us * 3e6), transcendentals=0)


def shape(dims, dtype):
    return jax.ShapeDtypeStruct(dims, dtype)


def whole(dims):
    return pl.BlockSpec(dims, lambda *_: (0,) * len(dims))


def exchange(outgo):
    recv = []
    for d, (axis, shift) in enumerate((("row", 1), ("row", -1), ("col", 1), ("col", -1))):
        size = lax.axis_size(axis)
        recv.append(lax.ppermute(outgo[d], axis, [(i, (i + shift) % size) for i in range(size)]))
    return recv


def per_device(
    iterate,
    residual,
    shadow,
    res_dirs,
    sol_dirs,
    omega_step,
    face_blocks,
    send_list,
    neighbour_perm,
    wall_perm,
    wall_count,
    wall_coef,
    rbf_support,
    rbf_weights,
):
    n_row, n_col = lax.axis_size("row"), lax.axis_size("col")
    sel_np = selection()
    sel = jnp.asarray(sel_np, BF16)
    selt = jnp.asarray(sel_np.T, BF16)
    cross = jnp.asarray(sel_np.T @ sel_np, BF16)
    spread = jnp.asarray(wall_spread(), BF16)
    eye = jnp.asarray(np.eye(E), BF16)

    one = pl.BlockSpec((1, E, BLOCK), lambda k: (k, 0, 0))
    pair = pl.BlockSpec((2, 1, E, BLOCK), lambda k: (0, k, 0, 0))
    lanes = pl.BlockSpec((SLOTS, STEP), lambda k: (0, k))
    dots, thi, tlo, outgo = call(
        basis_kernel,
        grid=(NOBJ,),
        in_specs=[SMEM, whole((4, H)), whole(sel.shape), one, pair, pair, whole((2, E, BLOCK))],
        out_specs=[
            pl.BlockSpec((1, 16, BLOCK), lambda k: (k, 0, 0)),
            lanes,
            lanes,
            pl.BlockSpec((4, H, STEP), lambda k: (0, 0, k)),
        ],
        out_shape=[
            shape((NOBJ, 16, BLOCK), F32),
            shape((SLOTS, WIDE), BF16),
            shape((SLOTS, WIDE), BF16),
            shape((4, H, WIDE), BF16),
        ],
        compiler_params=params(16),
        cost_estimate=cost(5),
        name="basis",
    )(omega_step, send_list, sel, residual, res_dirs, sol_dirs, shadow)
    recv = exchange(outgo)

    neighbour_perm, wall_perm, wall_count, wall_coef, omega_row, dots = lax.optimization_barrier(
        (neighbour_perm, wall_perm, wall_count, wall_coef, omega_step, dots)
    )
    slot = neighbour_perm.reshape(E, 4).T.reshape(FACES, 1)
    cidx = jnp.where(slot < SLOTS, slot, SLOTS + (slot % 4) * H + slot // 4 - H)
    row, col = lax.axis_index("row"), lax.axis_index("col")
    flags = jnp.stack([row > 0, row < n_row - 1, col > 0, col < n_col - 1]).astype(jnp.int32)
    live = jnp.arange(WMAX) < wall_count[0]
    wsel = (live[:, None] & (wall_perm[0, :WMAX, None] == jnp.arange(E))).astype(BF16)
    coef = wall_coef.reshape(3, NVAR, WMAX, 16).transpose(0, 2, 1, 3)
    coef = jnp.pad(coef[..., None], ((0, 0),) * 4 + ((0, 3),)).reshape(3, WMAX, BLOCK).astype(F32)
    om_row = jnp.pad(omega_row[None], ((0, 0), (0, LANES - NOBJ)))

    wt, q = call(
        blocks_kernel,
        grid=(4,),
        in_specs=[
            ANY,
            pl.BlockSpec((1, TRACE, TRACE, E), lambda f: (f, 0, 0, 0)),
            whole((2, E, BLOCK)),
            pl.BlockSpec((LANES, BLOCK), lambda f: (f, 0)),
            whole((E, E)),
        ],
        out_specs=[
            pl.BlockSpec((1, E, TRACE, TRACE), lambda f: (f, 0, 0, 0)),
            pl.BlockSpec((2, E, LANES), lambda f: (0, f, 0)),
        ],
        out_shape=[shape((4, E, TRACE, TRACE), BF16), shape((2, FACES, LANES), F32)],
        scratch_shapes=[pltpu.VMEM((E * TRACE, LANES), F32), pltpu.VMEM((2, TRACE, E), F32)],
        compiler_params=params(24),
        cost_estimate=cost(8),
        name="blocks",
    )(dots, face_blocks.transpose(1, 2, 3, 0), shadow, selt, eye)
    wt = wt.reshape(FACES, TRACE, TRACE)

    chunk = pl.BlockSpec((H, STEP), lambda k: (0, k))
    red = call(
        reduce_kernel,
        grid=(NOBJ,),
        in_specs=[SMEM, whole((FACES, 1)), lanes, lanes]
        + [chunk] * 4
        + [whole((2, FACES, LANES)), pl.BlockSpec((1, 16, BLOCK), lambda k: (k, 0, 0))],
        out_specs=whole((n_row, 16, LANES)),
        out_shape=shape((n_row, 16, LANES), F32),
        scratch_shapes=[
            pltpu.VMEM((FACES, 2 * SLOTS), BF16),
            pltpu.VMEM((16, LANES), F32),
            pltpu.VMEM((16, LANES), F32),
        ],
        compiler_params=params(16),
        cost_estimate=cost(3),
        name="reduce",
    )(flags, cidx, thi, tlo, *recv, q, dots)
    red_row = lax.all_to_all(red, "row", 0, 0, tiled=True)

    outgo2, yn = call(
        apply_kernel,
        in_specs=[SMEM] + [VMEM] * 10 + [ANY],
        out_specs=[VMEM, VMEM],
        out_shape=[shape((4, H, WIDE), BF16), shape((NVEC, 4, E, LANES), F32)],
        scratch_shapes=[pltpu.VMEM((FACES * VPAD, LANES), F32)] * 2,
        compiler_params=params(36),
        cost_estimate=cost(8),
        name="apply",
    )(flags, cidx, send_list, thi, tlo, *recv, wt, cross, red)
    recv2 = exchange(outgo2)

    red_row = call(
        merge_kernel,
        out_shape=shape((n_col, 16, LANES), F32),
        in_specs=[VMEM],
        out_specs=VMEM,
        compiler_params=params(2),
        name="merge",
    )(red_row)
    red = lax.all_to_all(red_row, "col", 0, 0, tiled=True)

    itout, base, st2, coefs, payload = call(
        step_kernel,
        grid=(NOBJ,),
        in_specs=[
            whole((n_col, 16, LANES)),
            whole((1, LANES)),
            one,
            pair,
            pair,
            one,
            pl.BlockSpec((NBAS, 4, E, LANES), lambda k: (k, 0, 0, 0)),
            whole(selt.shape),
            whole((WMAX, E)),
            whole((3, WMAX, BLOCK)),
            whole((BLOCK, LANES)),
        ],
        out_specs=[one, one, one, whole((8, LANES)), whole((n_row, NBLK * BPAD, LANES))],
        out_shape=[
            shape((NOBJ, E, BLOCK), F32),
            shape((NOBJ, E, BLOCK), F32),
            shape((NOBJ, E, BLOCK), F32),
            shape((8, LANES), F32),
            shape((n_row, NBLK * BPAD, LANES), BF16),
        ],
        scratch_shapes=[pltpu.VMEM((8, LANES), F32), pltpu.VMEM((NBLK * BPAD, LANES), F32)],
        compiler_params=params(16),
        cost_estimate=cost(5),
        name="step",
    )(red, om_row, residual, res_dirs, sol_dirs, iterate, yn, selt, wsel, coef, spread)
    sens = lax.all_to_all(payload, "row", 0, 0, tiled=True)

    resout = call(
        last_kernel,
        in_specs=[SMEM] + [VMEM] * 15 + [ANY],
        out_specs=VMEM,
        out_shape=shape((NOBJ, E, BLOCK), F32),
        scratch_shapes=[pltpu.VMEM((FACES * 8, LANES), F32)] * 2,
        compiler_params=params(32),
        cost_estimate=cost(8),
        name="last",
    )(flags, coefs, cidx, st2, base, *recv, *recv2, wt, sel, selt, payload)

    smoothed = call(
        smooth_kernel,
        in_specs=[SMEM, VMEM, VMEM],
        out_specs=VMEM,
        out_shape=shape((3 * NOBJ, NBLK * LANES), F32),
        scratch_shapes=[pltpu.VMEM((n_row * NBLK * BPAD, LANES), F32)],
        compiler_params=params(8),
        cost_estimate=cost(3),
        name="smooth",
    )(rbf_support, sens.reshape(-1, LANES), rbf_weights)
    return (itout, resout, smoothed)


def solution(mesh):
    both = ("row", "col")
    in_specs = (
        P(None, both, None),
        P(None, both, None),
        P(None, both, None),
        P(None, None, both, None),
        P(None, None, both, None),
        P(),
        P(both, None, None, None),
        P(both, None),
        P(both, None),
        P(both, None),
        P(both),
        P(None, None, both),
        P(both, None),
        P(both, None, None, None),
    )
    out_specs = (P(None, both, None), P(None, both, None), P(None, both))
    return jax.shard_map(
        per_device, mesh=mesh, in_specs=in_specs, out_specs=out_specs, check_vma=False
    )
```

```python
import jax
import jax.numpy as jnp
import numpy as np
from jax import lax
from jax.experimental import pallas as pl
from jax.experimental.pallas import tpu as pltpu
from jax.sharding import PartitionSpec as P

NVAR = 5
NOBJ = 6
E = 96
H = 48
WMAX = 48
BLOCK = 320
TRACE = 80
LANES = 128
NBLK = 6
NSUP = 4
NBAS = 3
NVEC = NOBJ * NBAS
WIDE = NVEC * LANES
STEP = NBAS * LANES
SLOTS = 4 * H
FACES = 4 * E
VPAD = 24
WPAD = TRACE + 1
BPAD = 24
F32 = jnp.float32
BF16 = jnp.bfloat16


def selection():
    sel = np.zeros((BLOCK, 4 * LANES), np.float32)
    for var in range(NVAR):
        for a in range(4):
            for c in range(4):
                i = var * 16 + a * 4 + c
                base = var * 64
                sel[base + 48 + a * 4 + c, 0 * LANES + i] = 1
                sel[base + a * 4 + c, 1 * LANES + i] = 1
                sel[base + a * 16 + 12 + c, 2 * LANES + i] = 1
                sel[base + a * 16 + c, 3 * LANES + i] = 1
    return sel


def wall_spread():
    out = np.zeros((BLOCK, NVAR * LANES), np.float32)
    for var in range(NVAR):
        for p in range(16):
            out[var * 64 + p * 4, var * LANES + p : (var + 1) * LANES : 16] = 1
    return out


def dot(a, b, dims=((1,), (0,))):
    return lax.dot_general(a, b, (dims, ((), ())), preferred_element_type=F32)


def split(x):
    high = x.astype(BF16)
    return high, (x - high.astype(F32)).astype(BF16)


def one_hot_rows(index, width):
    lane = lax.broadcasted_iota(jnp.int32, (index.shape[0], width), 1)
    return jnp.where(lane == index, 1.0, 0.0).astype(BF16)


def picker(elements):
    n = elements.shape[1]
    row = lax.broadcasted_iota(jnp.int32, (E, n), 0)
    return jnp.where(row == elements, 1.0, 0.0).T.astype(BF16)


def fetch(pairs, sems):
    copies = [pltpu.make_async_copy(a, b, sems.at[n]) for n, (a, b) in enumerate(pairs)]
    for copy in copies:
        copy.start()
    return copies


def wait(*copies):
    for copy in copies:
        copy.wait()


def basis_kernel(
    om_h, send_h, sel_h, r_h, d_h, s_h, sh_h, dots, table, us_h, o0, o1, o2, o3, om, send, sel, r, d, s, sh, us, sems, osems
):
    first = [(sel_h, sel), (sh_h, sh), (om_h, om), (send_h, send)]
    head = len(first)
    for k in range(NOBJ):
        first += [(r_h.at[k], r.at[k]), (d_h.at[:, k], d.at[:, k]), (s_h.at[:, k], s.at[:, k])]
    copies = fetch(first, sems)
    wait(*copies[:head])
    picks = [picker(send[f : f + 1, :]) for f in range(4)]
    stores = []
    for k in range(NOBJ):
        wait(*copies[head + 3 * k : head + 3 * k + 3])
        w = om[k]
        r0, d0, d1 = r[k], d[0, k], d[1, k]
        vecs = [w * r0, w * d0 + s[0, k], w * d1 + s[1, k]]
        for x, vec in enumerate([r0, d0, d1] + vecs):
            for i in range(2):
                dots[k, pl.ds(2 * x + i, 1), :] = jnp.sum(sh[i] * vec, axis=0, keepdims=True)
        dots[k, 12:16, :] = jnp.zeros((4, BLOCK), F32)
        for m, u in enumerate(vecs):
            us[k, m] = u
        stores += fetch([(us.at[k], us_h.at[k])], osems.at[k : k + 1])
        traces = dot(jnp.concatenate([u.astype(BF16) for u in vecs], axis=0), sel[...]).astype(BF16)
        at = slice(k * STEP, (k + 1) * STEP)
        for f, out in enumerate((o0, o1, o2, o3)):
            lanes = slice(f * LANES, (f + 1) * LANES)
            face = jnp.concatenate([traces[m * E : (m + 1) * E, lanes] for m in range(NBAS)], axis=1)
            table[f * H : (f + 1) * H, at] = face[H:]
            out[:, at] = dot(picks[f], face).astype(BF16)
    wait(*stores)


def blocks_kernel(_, b_h, sh_h, selt_h, wt_h, q, b, sh, selt, qscr, wide, packed, sems, osems):
    copies = fetch([(sh_h, sh), (selt_h, selt)] + [(b_h.at[f], b.at[f]) for f in range(4)], sems)
    wait(*copies[:2])
    parts = [split(sh[i]) for i in range(2)]
    nt = ((1,), (1,))
    stores = []
    for f in range(4):
        face = selt[f * LANES : (f + 1) * LANES, :]
        trsh = [(dot(face, high, nt) + dot(face, low, nt))[:TRACE] for high, low in parts]
        copies[2 + f].wait()

        def step(n, carry):
            for c in range(16):
                i = n * 16 + c
                x = b[f, i].astype(F32)
                for a in range(2):
                    qscr[a, pl.ds(i, 1), :] = jnp.sum(x * trsh[a], axis=0, keepdims=True)
                wide[pl.ds(i, E, stride=WPAD), 0:TRACE] = x.T
            return carry

        lax.fori_loop(0, TRACE // 16, step, 0)
        for a in range(2):
            q[a, f * E : (f + 1) * E, 0:TRACE] = qscr[a].T
            q[a, f * E : (f + 1) * E, TRACE:LANES] = jnp.zeros((E, LANES - TRACE), F32)

        def pack(n, carry):
            base = pl.multiple_of(n * 16 * WPAD, 8)
            for c in range(16):
                packed[f, n * 16 + c] = wide[pl.ds(base + c * WPAD, TRACE), 0:TRACE].astype(BF16)
            return carry

        lax.fori_loop(0, E // 16, pack, 0)
        stores += fetch([(packed.at[f], wt_h.at[f])], osems.at[f : f + 1])
    wait(*stores)


def received(flags, recv, at):
    return [jnp.where(flags[d] > 0, ref[:, at], jnp.zeros((), BF16)) for d, ref in enumerate(recv)]


def reduce_kernel(flags, cidx, table, r0, r1, r2, r3, q, dots, out, rows):
    hot = one_hot_rows(cidx[...], 2 * SLOTS)
    lane = lax.broadcasted_iota(jnp.int32, (16, LANES), 1)
    acc = jnp.zeros((16, LANES), F32)
    for k in range(NOBJ):
        at = slice(k * STEP, (k + 1) * STEP)
        full = jnp.concatenate(received(flags, (r0, r1, r2, r3), at) + [table[:, at]], axis=0)
        t = dot(hot, full)
        rows[k] = jnp.zeros((16, LANES), F32)
        for m in range(NBAS):
            for i in range(2):
                part = t[:, m * LANES : (m + 1) * LANES] * q[i]
                rows[k, pl.ds(6 + 2 * m + i, 1), :] = jnp.sum(part, axis=0, keepdims=True)
        col = jnp.sum(rows[k], axis=1, keepdims=True) + jnp.sum(dots[k], axis=1, keepdims=True)
        acc += jnp.where(lane == k, col, 0.0)
    out[...] = jnp.broadcast_to(acc[None], out.shape)


def merge_kernel(x, out):
    out[...] = jnp.broadcast_to(jnp.sum(x[...], axis=0, keepdims=True), out.shape)


def couple(t_ref, wt, y_ref, pad, f):
    unroll = 32

    def step(n, carry):
        for c in range(unroll):
            e = n * unroll + c
            at = pl.ds(pl.multiple_of((f * E + e) * pad, 8), pad)
            y_ref[at, 0:TRACE] = dot(t_ref[at, 0:TRACE].astype(BF16), wt[f, e])
        return carry

    lax.fori_loop(0, E // unroll, step, 0)


def apply_kernel(
    flags, cidx, send_h, table, r0, r1, r2, r3, wt_h, cross_h, _, o0, o1, o2, o3, yn_h, t_ref, y_ref, wt, send, cross, yn, out, sems, osems
):
    copies = fetch([(wt_h.at[f], wt.at[f]) for f in range(4)] + [(send_h, send), (cross_h, cross)], sems)
    hot = one_hot_rows(cidx[...], 2 * SLOTS)
    for k in range(NOBJ):
        at = slice(k * STEP, (k + 1) * STEP)
        full = jnp.concatenate(received(flags, (r0, r1, r2, r3), at) + [table[:, at]], axis=0)
        t = dot(hot, full)
        for f in range(4):
            for m in range(NBAS):
                rows = pl.ds(f * E * VPAD + k * NBAS + m, E, stride=VPAD)
                t_ref[rows, :] = t[f * E : (f + 1) * E, m * LANES : (m + 1) * LANES]
    for f in range(4):
        copies[f].wait()
        couple(t_ref, wt, y_ref, VPAD, f)
    wait(*copies[4:])
    picks = [picker(send[f : f + 1, :]) for f in range(4)]
    stores = []
    for k in range(NOBJ):
        total = None
        for f in range(4):
            ys = []
            for m in range(NBAS):
                y = y_ref[pl.ds(f * E * VPAD + k * NBAS + m, E, stride=VPAD), :][:, 0:TRACE]
                yn[k, m, f, :, 0:TRACE] = y
                ys.append(y.astype(BF16))
            part = dot(jnp.concatenate(ys, axis=0), cross[f * LANES : f * LANES + TRACE, :])
            total = part if total is None else total + part
        stores += fetch([(yn.at[k], yn_h.at[k])], osems.at[k : k + 1])
        total = total.astype(BF16)
        at = slice(k * STEP, (k + 1) * STEP)
        for f in range(4):
            lanes = slice(f * LANES, (f + 1) * LANES)
            face = jnp.concatenate([total[m * E : (m + 1) * E, lanes] for m in range(NBAS)], axis=1)
            out[f, :, at] = dot(picks[f], face).astype(BF16)
    stores += fetch([(out.at[f], o) for f, o in enumerate((o0, o1, o2, o3))], osems.at[NOBJ : NOBJ + 4])
    wait(*stores)


def solve(m00, m01, m10, m11, f0, f1):
    det = m00 * m11 - m01 * m10
    return (m11 * f0 - m01 * f1) / det, (m00 * f1 - m10 * f0) / det


def step_kernel(
    om, count, red, us_h, r_h, it_h, yn_h, wall, coef, selt_h, spread_h, itout_h, base_h, st2_h, coefs, payload, us, r, it, yn, selt, spread, itout, base, st2, scr, sems, osems
):
    first = [(selt_h, selt), (spread_h, spread)]
    for k in range(NOBJ):
        first += [(h.at[k], x.at[k]) for h, x in ((us_h, us), (yn_h, yn), (it_h, it), (r_h, r))]
    copies = fetch(first, sems)
    t = jnp.sum(red[...], axis=0)
    row = lambda n: t[n : n + 1]
    lane = lax.broadcasted_iota(jnp.int32, (1, LANES), 1)
    w = sum(jnp.where(lane == k, om[k], 0.0) for k in range(NOBJ))
    c0, c1 = solve(row(2), row(4), row(3), row(5), row(0), row(1))
    n0 = -(row(6) - c0 * row(8) - c1 * row(10))
    n1 = -(row(7) - c0 * row(9) - c1 * row(11))
    e0, e1 = solve(n0, row(4), n1, row(5), row(0) + n0, row(1) + n1)
    gamma = w * (1.0 - e0)
    delta = gamma + e0
    for n, x in enumerate([c0, c1, 1.0 - delta, delta * c0, delta * c1 - e1, gamma, w, w]):
        coefs[pl.ds(n, 1), :] = x
    scr[...] = jnp.zeros_like(scr)
    slots = lax.broadcasted_iota(jnp.int32, (1, WMAX), 1)
    pick = picker(jnp.where(slots < count[0], wall[:, 0:WMAX], E))
    slot = lax.broadcasted_iota(jnp.int32, (WMAX, LANES), 0) % 8
    group = lax.broadcasted_iota(jnp.int32, (WMAX, LANES), 1) // 16
    mine = slot == group
    wait(*copies[:2])
    stores = []
    for k in range(NOBJ):
        wait(*copies[2 + 4 * k : 6 + 4 * k])
        c = [coefs[n : n + 1, k : k + 1] for n in range(6)]
        u0, u1, u2 = (us[k, m] for m in range(NBAS))
        st1 = u0 - c[0] * u1 - c[1] * u2
        lift = None
        for f in range(4):
            y = yn[k, 0, f] - c[0] * yn[k, 1, f] - c[1] * yn[k, 2, f]
            high, low = split(y[:, 0:TRACE])
            block = selt[f * LANES : f * LANES + TRACE, :]
            part = dot(high, block) + dot(low, block)
            lift = part if lift is None else lift + part
        two = c[2] * u0 + c[3] * u1 + c[4] * u2 - c[5] * lift
        new = it[k] + st1 + two
        itout[k] = new
        st2[k] = two
        base[k] = r[k] - st1 - lift - two
        outs = [(x.at[k], h.at[k]) for x, h in ((itout, itout_h), (st2, st2_h), (base, base_h))]
        stores += fetch(outs, osems.at[3 * k : 3 * k + 3])
        high, low = split(new)
        high, low = split(dot(pick, high) + dot(pick, low))
        points = dot(high, spread[...]) + dot(low, spread[...])
        sums = [None] * 3
        for var in range(NVAR):
            part = points[:, var * LANES : (var + 1) * LANES]
            part = jnp.sum(jnp.where(mine, part, 0.0).reshape(NBLK, 8, LANES), axis=1)
            for a in range(3):
                term = coef[a * NVAR + var] * part
                sums[a] = term if sums[a] is None else sums[a] + term
        for a in range(3):
            scr[pl.ds(a * NOBJ + k, NBLK, stride=BPAD), :] = sums[a]
    payload[...] = jnp.broadcast_to(scr[...].astype(BF16)[None], payload.shape)
    wait(*stores)


def last_kernel(
    flags, coefs, cidx, st2_h, base_h, a0, a1, a2, a3, b0_h, b1_h, b2_h, b3_h, wt_h, sel_h, selt_h, w_h, _, out_h, weights, t_ref, y_ref, st2, base, b, wt, sel, selt, out, sems, osems
):
    first = [(sel_h, sel), (st2_h, st2)] + [(h, b.at[d]) for d, h in enumerate((b0_h, b1_h, b2_h, b3_h))]
    first += [(wt_h.at[f], wt.at[f]) for f in range(4)] + [(selt_h, selt), (base_h, base), (w_h, weights)]
    copies = fetch(first, sems)
    hot = one_hot_rows(cidx[...], 2 * SLOTS)
    wait(*copies[:6])
    for k in range(NOBJ):
        c = [coefs[n : n + 1, k : k + 1] for n in range(6)]
        rows = []
        for d, a in enumerate((a0, a1, a2, a3)):
            u = [a[:, (k * NBAS + m) * LANES : (k * NBAS + m + 1) * LANES].astype(F32) for m in range(3)]
            y = [b[d, :, (k * NBAS + m) * LANES : (k * NBAS + m + 1) * LANES].astype(F32) for m in range(3)]
            x = c[2] * u[0] + c[3] * u[1] + c[4] * u[2] - c[5] * (y[0] - c[0] * y[1] - c[1] * y[2])
            rows.append(jnp.where(flags[d] > 0, x, 0.0).astype(BF16))
        local = dot(st2[k, H:, :].astype(BF16), sel[...]).astype(BF16)
        rows += [local[:, f * LANES : (f + 1) * LANES] for f in range(4)]
        t = dot(hot, jnp.concatenate(rows, axis=0))
        for f in range(4):
            t_ref[pl.ds(f * E * 8 + k, E, stride=8), :] = t[f * E : (f + 1) * E]
    for f in range(4):
        copies[6 + f].wait()
        couple(t_ref, wt, y_ref, 8, f)
    wait(*copies[10:12])
    stores = []
    for k in range(NOBJ):
        lift = None
        for f in range(4):
            high, low = split(y_ref[pl.ds(f * E * 8 + k, E, stride=8), :][:, 0:TRACE])
            block = selt[f * LANES : f * LANES + TRACE, :]
            part = dot(high, block) + dot(low, block)
            lift = part if lift is None else lift + part
        out[k] = base[k] - lift
        stores += fetch([(out.at[k], out_h.at[k])], osems.at[k : k + 1])
    wait(*stores, *copies[12:])


def smooth_kernel(support, sens, weights, out, scr):
    scr[...] = sens[...].astype(F32)
    for m in range(NBLK):
        acc = None
        for s in range(NSUP):
            at = pl.multiple_of(support[m, s] * BPAD, 8)
            part = dot(scr[pl.ds(at, BPAD), :].astype(BF16), weights[m, s])
            acc = part if acc is None else acc + part
        out[:, m * LANES : (m + 1) * LANES] = acc[: 3 * NOBJ]


SMEM = pl.BlockSpec(memory_space=pltpu.SMEM)
ANY = pl.BlockSpec(memory_space=pl.ANY)
VMEM = pl.BlockSpec(memory_space=pltpu.VMEM)


def shape(dims, dtype):
    return jax.ShapeDtypeStruct(dims, dtype)


def far(x):
    return pltpu.with_memory_space_constraint(x, pltpu.HBM)


def near(x):
    return pltpu.with_memory_space_constraint(x, pltpu.VMEM)


def buffers(*arrays):
    return [pltpu.VMEM(x.shape, x.dtype) for x in arrays]


def local_call(kernel, name, us, mib, ins, outs, scratch):
    result = pl.pallas_call(
        kernel,
        in_specs=[spec for spec, _ in ins],
        out_specs=[spec for spec, _ in outs],
        out_shape=[x for _, x in outs],
        scratch_shapes=scratch,
        compiler_params=pltpu.CompilerParams(vmem_limit_bytes=mib << 20),
        cost_estimate=pl.CostEstimate(flops=int(us * 5e8), bytes_accessed=int(us * 1e6), transcendentals=0),
        name=name,
    )(*[x for _, x in ins])
    return result


def exchange(outgo):
    recv = []
    for d, (axis, shift) in enumerate((("row", 1), ("row", -1), ("col", 1), ("col", -1))):
        size = lax.axis_size(axis)
        recv.append(lax.ppermute(outgo[d], axis, [(i, (i + shift) % size) for i in range(size)]))
    return recv


def per_device(
    iterate,
    residual,
    shadow,
    res_dirs,
    sol_dirs,
    omega_step,
    face_blocks,
    send_list,
    neighbour_perm,
    wall_perm,
    wall_count,
    wall_coef,
    rbf_support,
    rbf_weights,
):
    n_row, n_col = lax.axis_size("row"), lax.axis_size("col")
    sel_np = selection()
    sel = jnp.asarray(sel_np, BF16)
    selt = jnp.asarray(sel_np.T, BF16)
    cross = jnp.asarray(sel_np.T @ sel_np, BF16)
    spread = jnp.asarray(wall_spread(), BF16)
    sem = pltpu.SemaphoreType.DMA
    fields = (NOBJ, E, BLOCK)
    traces = pltpu.VMEM((H, WIDE), BF16)

    big = (4, E, TRACE, TRACE)
    spare = (NOBJ, NBAS, 4, E, LANES)
    basis = (NOBJ, NBAS, E, BLOCK)

    dots, table, us, *outgo = local_call(
        basis_kernel,
        "basis",
        5,
        24,
        [(ANY, far(x)) for x in (omega_step, send_list, sel, residual, res_dirs, sol_dirs, shadow)],
        [
            (VMEM, pltpu.VMEM((NOBJ, 16, BLOCK), F32)),
            (VMEM, pltpu.VMEM((SLOTS, WIDE), BF16)),
            (ANY, pltpu.HBM(basis, F32)),
        ]
        + [(VMEM, traces)] * 4,
        [pltpu.SMEM((NOBJ,), F32)]
        + buffers(send_list, sel, residual, res_dirs, sol_dirs, shadow)
        + [pltpu.VMEM(basis, F32), sem((4 + 3 * NOBJ,)), sem((NOBJ,))],
    )
    recv = exchange(outgo)

    neighbour_perm, wall_coef, dots = lax.optimization_barrier((neighbour_perm, wall_coef, dots))
    slot = neighbour_perm.reshape(E, 4).T.reshape(FACES, 1)
    cidx = jnp.where(slot < SLOTS, slot, SLOTS + (slot % 4) * H + slot // 4 - H)
    row, col = lax.axis_index("row"), lax.axis_index("col")
    flags = jnp.stack([row > 0, row < n_row - 1, col > 0, col < n_col - 1]).astype(jnp.int32)
    coef = wall_coef.reshape(3 * NVAR, NBLK, LANES).astype(F32)

    blocks = face_blocks.transpose(1, 2, 3, 0)
    wt, q = local_call(
        blocks_kernel,
        "blocks",
        8,
        28,
        [(VMEM, near(dots)), (ANY, far(blocks)), (ANY, far(shadow)), (ANY, far(selt))],
        [(ANY, pltpu.HBM(big, BF16)), (VMEM, pltpu.VMEM((2, FACES, LANES), F32))],
        buffers(blocks, shadow, selt)
        + [
            pltpu.VMEM((2, TRACE, E), F32),
            pltpu.VMEM((E * WPAD, LANES), F32),
            pltpu.VMEM(big, BF16),
            sem((6,)),
            sem((4,)),
        ],
    )

    tables = [(VMEM, near(table))] + [(VMEM, near(x)) for x in recv]
    (red,) = local_call(
        reduce_kernel,
        "reduce",
        3,
        12,
        [(SMEM, flags), (VMEM, near(cidx))] + tables + [(VMEM, near(q)), (VMEM, near(dots))],
        [(VMEM, shape((n_row, 16, LANES), F32))],
        [pltpu.VMEM((NOBJ, 16, LANES), F32)],
    )
    red_row = lax.all_to_all(red, "row", 0, 0, tiled=True)

    *outgo2, yn = local_call(
        apply_kernel,
        "apply",
        8,
        40,
        [(SMEM, flags), (VMEM, near(cidx)), (ANY, far(send_list))]
        + tables
        + [(ANY, far(wt)), (ANY, far(cross)), (ANY, red)],
        [(ANY, pltpu.HBM((H, WIDE), BF16))] * 4 + [(ANY, pltpu.HBM(spare, F32))],
        [pltpu.VMEM((FACES * VPAD, LANES), F32)] * 2
        + [pltpu.VMEM(big, BF16)]
        + buffers(send_list, cross)
        + [pltpu.VMEM(spare, F32), pltpu.VMEM((4, H, WIDE), BF16), sem((6,)), sem((NOBJ + 4,))],
    )
    recv2 = exchange(outgo2)

    (red_row,) = local_call(
        merge_kernel, "merge", 1, 4, [(VMEM, red_row)], [(VMEM, shape((n_col, 16, LANES), F32))], []
    )
    red = lax.all_to_all(red_row, "col", 0, 0, tiled=True)

    payload = (n_row, NBLK * BPAD, LANES)
    itout, base, st2, coefs, payload = local_call(
        step_kernel,
        "step",
        5,
        32,
        [(SMEM, omega_step), (SMEM, wall_count), (VMEM, red)]
        + [(ANY, far(x)) for x in (us, residual, iterate, yn)]
        + [(VMEM, wall_perm), (VMEM, near(coef)), (ANY, far(selt)), (ANY, far(spread))],
        [(ANY, shape(fields, F32))]
        + [(ANY, pltpu.HBM(fields, F32))] * 2
        + [(VMEM, pltpu.VMEM((8, LANES), F32)), (VMEM, shape(payload, BF16))],
        [pltpu.VMEM(basis, F32)]
        + buffers(residual, iterate)
        + [pltpu.VMEM(spare, F32)]
        + buffers(selt, spread)
        + [pltpu.VMEM(fields, F32)] * 3
        + [pltpu.VMEM((NBLK * BPAD, LANES), F32), sem((2 + 4 * NOBJ,)), sem((3 * NOBJ,))],
    )
    sens = lax.all_to_all(payload, "row", 0, 0, tiled=True)

    resout, weights = local_call(
        last_kernel,
        "last",
        6,
        28,
        [(SMEM, flags), (VMEM, near(coefs)), (VMEM, near(cidx)), (ANY, far(st2)), (ANY, far(base))]
        + [(VMEM, near(x)) for x in recv]
        + [(ANY, far(x)) for x in recv2 + [wt, sel, selt, rbf_weights]]
        + [(ANY, payload)],
        [(ANY, shape(fields, F32)), (VMEM, pltpu.VMEM(rbf_weights.shape, BF16))],
        [pltpu.VMEM((FACES * 8, LANES), F32)] * 2
        + [pltpu.VMEM(fields, F32)] * 2
        + [pltpu.VMEM((4, H, WIDE), BF16), pltpu.VMEM(big, BF16)]
        + buffers(sel, selt, residual)
        + [sem((13,)), sem((NOBJ,))],
    )

    (smoothed,) = local_call(
        smooth_kernel,
        "smooth",
        2,
        8,
        [(SMEM, rbf_support), (VMEM, sens.reshape(-1, LANES)), (VMEM, near(weights))],
        [(VMEM, shape((3 * NOBJ, NBLK * LANES), F32))],
        [pltpu.VMEM((n_row * NBLK * BPAD, LANES), F32)],
    )
    return (itout, resout, smoothed)


def solution(mesh):
    both = ("row", "col")
    in_specs = (
        P(None, both, None),
        P(None, both, None),
        P(None, both, None),
        P(None, None, both, None),
        P(None, None, both, None),
        P(),
        P(both, None, None, None),
        P(both, None),
        P(both, None),
        P(both, None),
        P(both),
        P(None, None, both),
        P(both, None),
        P(both, None, None, None),
    )
    out_specs = (P(None, both, None), P(None, both, None), P(None, both))
    return jax.shard_map(
        per_device, mesh=mesh, in_specs=in_specs, out_specs=out_specs, check_vma=False
    )
```

```python
import jax
import jax.numpy as jnp
import numpy as np
from jax import lax
from jax.experimental import pallas as pl
from jax.experimental.pallas import tpu as pltpu
from jax.sharding import PartitionSpec as P

NVAR = 5
NOBJ = 6
E = 96
H = 48
WMAX = 48
BLOCK = 320
TRACE = 80
LANES = 128
NBLK = 6
NSUP = 4
NBAS = 3
NVEC = NOBJ * NBAS
WIDE = NVEC * LANES
STEP = NBAS * LANES
SLOTS = 4 * H
FACES = 4 * E
VPAD = 24
WPAD = TRACE + 1
BPAD = 24
F32 = jnp.float32
BF16 = jnp.bfloat16


def selection():
    sel = np.zeros((BLOCK, 4 * LANES), np.float32)
    for var in range(NVAR):
        for a in range(4):
            for c in range(4):
                i = var * 16 + a * 4 + c
                base = var * 64
                sel[base + 48 + a * 4 + c, 0 * LANES + i] = 1
                sel[base + a * 4 + c, 1 * LANES + i] = 1
                sel[base + a * 16 + 12 + c, 2 * LANES + i] = 1
                sel[base + a * 16 + c, 3 * LANES + i] = 1
    return sel


def wall_spread():
    out = np.zeros((BLOCK, NVAR * LANES), np.float32)
    for var in range(NVAR):
        for p in range(16):
            out[var * 64 + p * 4, var * LANES + p : (var + 1) * LANES : 16] = 1
    return out


def dot(a, b, dims=((1,), (0,))):
    return lax.dot_general(a, b, (dims, ((), ())), preferred_element_type=F32)


def split(x):
    high = x.astype(BF16)
    return high, (x - high.astype(F32)).astype(BF16)


def picker(elements):
    n = elements.shape[1]
    row = lax.broadcasted_iota(jnp.int32, (E, n), 0)
    return jnp.where(row == elements, 1.0, 0.0).T.astype(BF16)


def fetch(pairs, sems):
    copies = [pltpu.make_async_copy(a, b, sems.at[n]) for n, (a, b) in enumerate(pairs)]
    for copy in copies:
        copy.start()
    return copies


def wait(*copies):
    for copy in copies:
        copy.wait()


def basis_kernel(
    flags, om_h, send_h, sel_h, r_h, d_h, s_h, sh_h, dots, table, us_h, o0, o1, o2, o3, om, send, sel, r, d, s, sh, us, sems, osems
):
    first = [(sel_h, sel), (sh_h, sh), (om_h, om), (send_h, send)]
    head = len(first)
    for k in range(NOBJ):
        first += [(r_h.at[k], r.at[k]), (d_h.at[:, k], d.at[:, k]), (s_h.at[:, k], s.at[:, k])]
    copies = fetch(first, sems)
    wait(*copies[:head])
    picks = [picker(send[f : f + 1, :]) for f in range(4)]
    stores = []
    for k in range(NOBJ):
        wait(*copies[head + 3 * k : head + 3 * k + 3])
        w = om[k]
        r0, d0, d1 = r[k], d[0, k], d[1, k]
        vecs = [w * r0, w * d0 + s[0, k], w * d1 + s[1, k]]
        for x, vec in enumerate([r0, d0, d1] + vecs):
            for i in range(2):
                dots[k, pl.ds(2 * x + i, 1), :] = jnp.sum(sh[i] * vec, axis=0, keepdims=True)
        dots[k, 12:16, :] = jnp.zeros((4, BLOCK), F32)
        for m, u in enumerate(vecs):
            us[k, m] = u
        stores += fetch([(us.at[k], us_h.at[k])], osems.at[k : k + 1])
        traces = dot(jnp.concatenate([u.astype(BF16) for u in vecs], axis=0), sel[...]).astype(BF16)
        at = slice(k * STEP, (k + 1) * STEP)
        for f, out in enumerate((o0, o1, o2, o3)):
            lanes = slice(f * LANES, (f + 1) * LANES)
            face = jnp.concatenate([traces[m * E : (m + 1) * E, lanes] for m in range(NBAS)], axis=1)
            table[f * H : (f + 1) * H, at] = face[H:]
            out[:, at] = dot(picks[f], face).astype(BF16)
    wait(*stores)


def relayout(b, f, wt, base, i, each=None):
    x = b[f, i].astype(F32)
    if each is not None:
        each(i, x)
    wt[pl.ds(base + i, E, stride=WPAD), 0:TRACE] = x.T


def blocks_kernel(_, perm_h, b_h, sh_h, selt_h, wt, q, hot, b, sh, selt, perm, qscr, square, sems):
    first = [(sh_h, sh), (selt_h, selt), (perm_h, perm)]
    copies = fetch(first + [(b_h.at[f], b.at[f]) for f in range(4)], sems)
    wait(*copies[:3])
    slot = perm[...]
    entry = jnp.where(slot < SLOTS, slot, SLOTS + (slot & 3) * H + (slot >> 2) - H)
    row = lax.broadcasted_iota(jnp.int32, (2 * SLOTS, FACES), 0)
    marks = jnp.where(row == entry, 1.0, 0.0).T
    for n in range(3):
        square[n] = marks[:, n * LANES : (n + 1) * LANES]
    parts = [split(sh[i]) for i in range(2)]
    nt = ((1,), (1,))
    for f in range(4):
        for n in range(3):
            lanes = slice(n * LANES, (n + 1) * LANES)
            hot[f * E : (f + 1) * E, lanes] = square[n, pl.ds(f, E, stride=4), :].astype(BF16)
        face = selt[f * LANES : (f + 1) * LANES, :]
        trsh = [(dot(face, high, nt) + dot(face, low, nt))[:TRACE] for high, low in parts]
        copies[3 + f].wait()

        def couple_shadow(i, x):
            for a in range(2):
                qscr[a, pl.ds(i, 1), :] = jnp.sum(x * trsh[a], axis=0, keepdims=True)

        for i in range(TRACE):
            relayout(b, f, wt, f * E * WPAD, i, couple_shadow)
        for a in range(2):
            q[a, f * E : (f + 1) * E, 0:TRACE] = qscr[a].T
            q[a, f * E : (f + 1) * E, TRACE:LANES] = jnp.zeros((E, LANES - TRACE), F32)


def received(flags, recv, at):
    return [jnp.where(flags[d] > 0, ref[:, at], jnp.zeros((), BF16)) for d, ref in enumerate(recv)]


def merge_kernel(x, _, out):
    out[...] = jnp.broadcast_to(jnp.sum(x[...], axis=0, keepdims=True), out.shape)


def couple(t_ref, wt, base, y_ref, pad, face, e):
    at = pl.ds(face * pad, pad)
    block = wt[pl.ds(base + e * WPAD, TRACE), 0:TRACE].astype(BF16)
    y_ref[at, 0:TRACE] = dot(t_ref[at, 0:TRACE].astype(BF16), block)


def face_rows(y_ref, row, pad):
    return jnp.concatenate([y_ref[pl.ds(f * E * pad + row, E, stride=pad), :] for f in range(4)], axis=1)


def lifted(y, selt):
    high, low = split(y)
    both = dot(jnp.concatenate([high, low], axis=0), selt[...])
    return both[:E] + both[E:]


def apply_kernel(
    flags, hot, table, r0, r1, r2, r3, q, dots, wt, red, yn_h, rows, t_ref, y_ref, yn, osems
):
    y_ref[...] = jnp.zeros_like(y_ref)
    lane = lax.broadcasted_iota(jnp.int32, (16, LANES), 1)
    acc = jnp.zeros((16, LANES), F32)
    for k in range(NOBJ):
        at = slice(k * STEP, (k + 1) * STEP)
        full = jnp.concatenate(received(flags, (r0, r1, r2, r3), at) + [table[:, at]], axis=0)
        t = dot(hot[...], full)
        rows[k] = jnp.zeros((16, LANES), F32)
        for m in range(NBAS):
            part = t[:, m * LANES : (m + 1) * LANES]
            for f in range(4):
                to = pl.ds(f * E * VPAD + k * NBAS + m, E, stride=VPAD)
                t_ref[to, :] = part[f * E : (f + 1) * E]
            for i in range(2):
                rows[k, pl.ds(6 + 2 * m + i, 1), :] = jnp.sum(part * q[i], axis=0, keepdims=True)
        col = jnp.sum(rows[k], axis=1, keepdims=True) + jnp.sum(dots[k], axis=1, keepdims=True)
        acc += jnp.where(lane == k, col, 0.0)
    red[...] = jnp.broadcast_to(acc[None], red.shape)
    for face in range(FACES):
        couple(t_ref, wt, face // E * E * WPAD, y_ref, VPAD, face, face % E)
    stores = []
    for k in range(NOBJ):
        for m in range(NBAS):
            y = face_rows(y_ref, k * NBAS + m, VPAD)
            for f in range(4):
                yn[k, m, f] = y[:, f * LANES : (f + 1) * LANES]
        stores += fetch([(yn.at[k], yn_h.at[k])], osems.at[k : k + 1])
    wait(*stores)


def outgo_kernel(_, yn_h, send_h, cross_h, o0, o1, o2, o3, yn, send, cross, out, sems, osems):
    first = [(send_h, send), (cross_h, cross)] + [(yn_h.at[k], yn.at[k]) for k in range(NOBJ)]
    copies = fetch(first, sems)
    wait(*copies[:2])
    picks = [picker(send[f : f + 1, :]) for f in range(4)]
    for k in range(NOBJ):
        copies[2 + k].wait()
        ys = [jnp.concatenate([yn[k, m, f].astype(BF16) for f in range(4)], axis=1) for m in range(NBAS)]
        total = dot(jnp.concatenate(ys, axis=0), cross[...]).astype(BF16)
        at = slice(k * STEP, (k + 1) * STEP)
        for f in range(4):
            lanes = slice(f * LANES, (f + 1) * LANES)
            face = jnp.concatenate([total[m * E : (m + 1) * E, lanes] for m in range(NBAS)], axis=1)
            out[f, :, at] = dot(picks[f], face).astype(BF16)
    wait(*fetch([(out.at[f], o) for f, o in enumerate((o0, o1, o2, o3))], osems))


def solve(m00, m01, m10, m11, f0, f1):
    det = m00 * m11 - m01 * m10
    return (m11 * f0 - m01 * f1) / det, (m00 * f1 - m10 * f0) / det


def step_kernel(
    om, count, red, us_h, it_h, yn_h, wall, coef, selt_h, spread_h, itout_h, base_h, st2_h, coefs, payload, us, it, yn, selt, spread, itout, base, st2, points, scr, sems, osems
):
    first = [(selt_h, selt)]
    for k in range(NOBJ):
        first += [(h.at[k], x.at[k]) for h, x in ((us_h, us), (yn_h, yn), (it_h, it))]
    copies = fetch(first + [(spread_h, spread)], sems)
    t = jnp.sum(red[...], axis=0)
    row = lambda n: t[n : n + 1]
    lane = lax.broadcasted_iota(jnp.int32, (1, LANES), 1)
    w = sum(jnp.where(lane == k, om[k], 0.0) for k in range(NOBJ))
    c0, c1 = solve(row(2), row(4), row(3), row(5), row(0), row(1))
    n0 = -(row(6) - c0 * row(8) - c1 * row(10))
    n1 = -(row(7) - c0 * row(9) - c1 * row(11))
    e0, e1 = solve(n0, row(4), n1, row(5), row(0) + n0, row(1) + n1)
    gamma = w * (1.0 - e0)
    delta = gamma + e0
    for n, x in enumerate([c0, c1, 1.0 - delta, delta * c0, delta * c1 - e1, gamma, 1.0 / w, w]):
        coefs[pl.ds(n, 1), :] = x
    scr[...] = jnp.zeros_like(scr)
    slots = lax.broadcasted_iota(jnp.int32, (1, WMAX), 1)
    pick = picker(jnp.where(slots < count[0], wall[:, 0:WMAX], E))
    slot = lax.broadcasted_iota(jnp.int32, (WMAX, LANES), 0) % 8
    group = lax.broadcasted_iota(jnp.int32, (WMAX, LANES), 1) // 16
    mine = slot == group
    copies[0].wait()
    stores = []
    half = NOBJ * WMAX
    for k in range(NOBJ):
        wait(*copies[1 + 3 * k : 4 + 3 * k])
        c = [coefs[n : n + 1, k : k + 1] for n in range(7)]
        u0, u1, u2 = (us[k, m] for m in range(NBAS))
        st1 = u0 - c[0] * u1 - c[1] * u2
        y = [yn[k, 0, f] - c[0] * yn[k, 1, f] - c[1] * yn[k, 2, f] for f in range(4)]
        lift = lifted(jnp.concatenate(y, axis=1), selt)
        two = c[2] * u0 + c[3] * u1 + c[4] * u2 - c[5] * lift
        both = st1 + two
        new = it[k] + both
        itout[k] = new
        st2[k] = two[H:]
        base[k] = c[6] * u0 - both - lift
        outs = [(x.at[k], h.at[k]) for x, h in ((itout, itout_h), (st2, st2_h), (base, base_h))]
        stores += fetch(outs, osems.at[3 * k : 3 * k + 3])
        high, low = split(new)
        high, low = split(dot(pick, high) + dot(pick, low))
        points[k * WMAX : (k + 1) * WMAX, :] = high
        points[half + k * WMAX : half + (k + 1) * WMAX, :] = low
    copies[-1].wait()
    every = dot(points[...], spread[...])
    for k in range(NOBJ):
        at = slice(k * WMAX, (k + 1) * WMAX)
        below = slice(half + k * WMAX, half + (k + 1) * WMAX)
        wide = every[at] + every[below]
        sums = [None] * 3
        for var in range(NVAR):
            part = wide[:, var * LANES : (var + 1) * LANES]
            part = jnp.sum(jnp.where(mine, part, 0.0).reshape(NBLK, 8, LANES), axis=1)
            for a in range(3):
                term = coef[a * NVAR + var] * part
                sums[a] = term if sums[a] is None else sums[a] + term
        for a in range(3):
            scr[pl.ds(a * NOBJ + k, NBLK, stride=BPAD), :] = sums[a]
    payload[...] = jnp.broadcast_to(scr[...].astype(BF16)[None], payload.shape)
    wait(*stores)


def last_kernel(
    flags, coefs, hot, st2_h, base_h, a0, a1, a2, a3, b0_h, b1_h, b2_h, b3_h, blocks_h, sel_h, selt_h, w_h, _, out_h, weights, t_ref, y_ref, st2, base, b, blocks, w0, w1, w2, w3, sel, selt, out, sems, osems
):
    first = [(sel_h, sel), (st2_h, st2)] + [(h, b.at[d]) for d, h in enumerate((b0_h, b1_h, b2_h, b3_h))]
    first += [(blocks_h.at[f], blocks.at[f]) for f in range(4)] + [(selt_h, selt), (base_h, base), (w_h, weights)]
    copies = fetch(first, sems)
    y_ref[...] = jnp.zeros_like(y_ref)
    wait(*copies[:6])
    for k in range(NOBJ):
        c = [coefs[n : n + 1, k : k + 1] for n in range(6)]
        rows = []
        for d, a in enumerate((a0, a1, a2, a3)):
            u = [a[:, (k * NBAS + m) * LANES : (k * NBAS + m + 1) * LANES].astype(F32) for m in range(3)]
            y = [b[d, :, (k * NBAS + m) * LANES : (k * NBAS + m + 1) * LANES].astype(F32) for m in range(3)]
            x = c[2] * u[0] + c[3] * u[1] + c[4] * u[2] - c[5] * (y[0] - c[0] * y[1] - c[1] * y[2])
            rows.append(jnp.where(flags[d] > 0, x, 0.0).astype(BF16))
        local = dot(st2[k].astype(BF16), sel[...]).astype(BF16)
        rows += [local[:, f * LANES : (f + 1) * LANES] for f in range(4)]
        t = dot(hot[...], jnp.concatenate(rows, axis=0))
        for f in range(4):
            t_ref[pl.ds(f * E * 8 + k, E, stride=8), :] = t[f * E : (f + 1) * E]
    wts = (w0, w1, w2, w3)
    rounds = 16
    for f in range(5):
        if f < 4:
            copies[6 + f].wait()
        for n in range(rounds):
            for c in range(TRACE // rounds):
                if f < 4:
                    relayout(blocks, f, wts[f], 0, n * (TRACE // rounds) + c)
            for c in range(E // rounds):
                if f > 0:
                    e = n * (E // rounds) + c
                    couple(t_ref, wts[f - 1], 0, y_ref, 8, (f - 1) * E + e, e)
    wait(*copies[10:12])
    stores = []
    for k in range(NOBJ):
        out[k] = base[k] - lifted(face_rows(y_ref, k, 8), selt)
        stores += fetch([(out.at[k], out_h.at[k])], osems.at[k : k + 1])
    wait(*stores, *copies[12:])


def smooth_kernel(support, sens, weights, out, scr):
    scr[...] = sens[...].astype(F32)
    for m in range(NBLK):
        acc = None
        for s in range(NSUP):
            at = pl.multiple_of(support[m, s] * BPAD, 8)
            part = dot(scr[pl.ds(at, BPAD), :].astype(BF16), weights[m, s])
            acc = part if acc is None else acc + part
        out[:, m * LANES : (m + 1) * LANES] = acc[: 3 * NOBJ]


SMEM = pl.BlockSpec(memory_space=pltpu.SMEM)
ANY = pl.BlockSpec(memory_space=pl.ANY)
VMEM = pl.BlockSpec(memory_space=pltpu.VMEM)


def shape(dims, dtype):
    return jax.ShapeDtypeStruct(dims, dtype)


def far(x):
    return pltpu.with_memory_space_constraint(x, pltpu.HBM)


def near(x):
    return pltpu.with_memory_space_constraint(x, pltpu.VMEM)


def buffers(*arrays):
    return [pltpu.VMEM(x.shape, x.dtype) for x in arrays]


def local_call(kernel, name, us, mib, ins, outs, scratch):
    result = pl.pallas_call(
        kernel,
        in_specs=[spec for spec, _ in ins],
        out_specs=[spec for spec, _ in outs],
        out_shape=[x for _, x in outs],
        scratch_shapes=scratch,
        compiler_params=pltpu.CompilerParams(vmem_limit_bytes=mib << 20),
        cost_estimate=pl.CostEstimate(flops=int(us * 5e8), bytes_accessed=int(us * 1e6), transcendentals=0),
        name=name,
    )(*[x for _, x in ins])
    return result


def exchange(outgo):
    recv = []
    for d, (axis, shift) in enumerate((("row", 1), ("row", -1), ("col", 1), ("col", -1))):
        size = lax.axis_size(axis)
        recv.append(lax.ppermute(outgo[d], axis, [(i, (i + shift) % size) for i in range(size)]))
    return recv


def per_device(
    iterate,
    residual,
    shadow,
    res_dirs,
    sol_dirs,
    omega_step,
    face_blocks,
    send_list,
    neighbour_perm,
    wall_perm,
    wall_count,
    wall_coef,
    rbf_support,
    rbf_weights,
):
    n_row, n_col = lax.axis_size("row"), lax.axis_size("col")
    sel_np = selection()
    sel = jnp.asarray(sel_np, BF16)
    selt = jnp.asarray(sel_np.T, BF16)
    cross = jnp.asarray(sel_np.T @ sel_np, BF16)
    spread = jnp.asarray(wall_spread(), BF16)
    sem = pltpu.SemaphoreType.DMA
    fields = (NOBJ, E, BLOCK)
    traces = pltpu.VMEM((H, WIDE), BF16)

    spare = (NOBJ, NBAS, 4, E, LANES)
    basis = (NOBJ, NBAS, E, BLOCK)

    row, col = lax.axis_index("row"), lax.axis_index("col")
    flags = jnp.stack([row > 0, row < n_row - 1, col > 0, col < n_col - 1]).astype(jnp.int32)
    dots, table, us, *outgo = local_call(
        basis_kernel,
        "basis",
        5,
        24,
        [(SMEM, flags)]
        + [(ANY, far(x)) for x in (omega_step, send_list, sel, residual, res_dirs, sol_dirs, shadow)],
        [
            (VMEM, pltpu.VMEM((NOBJ, 16, BLOCK), F32)),
            (VMEM, pltpu.VMEM((SLOTS, WIDE), BF16)),
            (ANY, pltpu.HBM(basis, F32)),
        ]
        + [(VMEM, traces)] * 4,
        [pltpu.SMEM((NOBJ,), F32)]
        + buffers(send_list, sel, residual, res_dirs, sol_dirs, shadow)
        + [pltpu.VMEM(basis, F32), sem((4 + 3 * NOBJ,)), sem((NOBJ,))],
    )
    recv = exchange(outgo)

    blocks = face_blocks.transpose(1, 2, 3, 0)
    wt, q, hot = local_call(
        blocks_kernel,
        "blocks",
        6,
        12,
        [(VMEM, near(dots))] + [(ANY, far(x)) for x in (neighbour_perm, blocks, shadow, selt)],
        [
            (VMEM, pltpu.VMEM((FACES * WPAD, LANES), F32)),
            (VMEM, pltpu.VMEM((2, FACES, LANES), F32)),
            (VMEM, pltpu.VMEM((FACES, 2 * SLOTS), BF16)),
        ],
        buffers(blocks, shadow, selt, neighbour_perm)
        + [pltpu.VMEM((2, TRACE, E), F32), pltpu.VMEM((3, FACES, LANES), F32), sem((7,))],
    )

    red, yn = local_call(
        apply_kernel,
        "apply",
        7,
        24,
        [(SMEM, flags), (VMEM, near(hot)), (VMEM, near(table))]
        + [(VMEM, near(x)) for x in recv + [q, dots, wt]],
        [(VMEM, shape((n_row, 16, LANES), F32)), (ANY, pltpu.HBM(spare, F32))],
        [pltpu.VMEM((NOBJ, 16, LANES), F32)]
        + [pltpu.VMEM((FACES * VPAD, LANES), F32)] * 2
        + [pltpu.VMEM(spare, F32), sem((NOBJ,))],
    )
    outgo2 = local_call(
        outgo_kernel,
        "outgo",
        4,
        12,
        [(ANY, red)] + [(ANY, far(x)) for x in (yn, send_list, cross)],
        [(ANY, pltpu.HBM((H, WIDE), BF16))] * 4,
        [pltpu.VMEM(spare, F32)]
        + buffers(send_list, cross)
        + [pltpu.VMEM((4, H, WIDE), BF16), sem((2 + NOBJ,)), sem((4,))],
    )
    recv2 = exchange(outgo2)
    red_row = lax.all_to_all(red, "row", 0, 0, tiled=True)
    wall_coef, wall_perm, wall_count, rbf_support, red = lax.optimization_barrier(
        (wall_coef, wall_perm, wall_count, rbf_support, red)
    )
    coef = wall_coef.reshape(3 * NVAR, NBLK, LANES).astype(F32)
    (red_row,) = local_call(
        merge_kernel, "merge", 1, 4, [(VMEM, red_row), (ANY, far(outgo2[0]))], [(VMEM, shape((n_col, 16, LANES), F32))], []
    )
    red = lax.all_to_all(red_row, "col", 0, 0, tiled=True)

    payload = (n_row, NBLK * BPAD, LANES)
    upper = (NOBJ, E - H, BLOCK)
    itout, base, st2, coefs, payload = local_call(
        step_kernel,
        "step",
        6,
        32,
        [(SMEM, omega_step), (SMEM, wall_count), (VMEM, red)]
        + [(ANY, far(x)) for x in (us, iterate, yn)]
        + [(VMEM, wall_perm), (VMEM, near(coef)), (ANY, far(selt)), (ANY, far(spread))],
        [(ANY, shape(fields, F32)), (ANY, pltpu.HBM(fields, F32)), (ANY, pltpu.HBM(upper, F32))]
        + [(VMEM, pltpu.VMEM((8, LANES), F32)), (VMEM, shape(payload, BF16))],
        [pltpu.VMEM(basis, F32)]
        + buffers(iterate)
        + [pltpu.VMEM(spare, F32)]
        + buffers(selt, spread)
        + [pltpu.VMEM(fields, F32)] * 2
        + [pltpu.VMEM(upper, F32), pltpu.VMEM((2 * NOBJ * WMAX, BLOCK), BF16)]
        + [pltpu.VMEM((NBLK * BPAD, LANES), F32), sem((2 + 3 * NOBJ,)), sem((3 * NOBJ,))],
    )
    payload, *recv2 = lax.optimization_barrier((payload, *recv2))
    sens = lax.all_to_all(payload, "row", 0, 0, tiled=True)

    resout, weights = local_call(
        last_kernel,
        "last",
        8,
        40,
        [(SMEM, flags), (VMEM, near(coefs)), (VMEM, near(hot)), (ANY, far(st2)), (ANY, far(base))]
        + [(VMEM, near(x)) for x in recv]
        + [(ANY, far(x)) for x in recv2 + [blocks, sel, selt, rbf_weights]]
        + [(ANY, payload)],
        [(ANY, shape(fields, F32)), (VMEM, pltpu.VMEM(rbf_weights.shape, BF16))],
        [pltpu.VMEM((FACES * 8, LANES), F32)] * 2
        + [pltpu.VMEM(upper, F32), pltpu.VMEM(fields, F32), pltpu.VMEM((4, H, WIDE), BF16)]
        + buffers(blocks)
        + [pltpu.VMEM((E * WPAD, LANES), F32)] * 4
        + buffers(sel, selt, residual)
        + [sem((13,)), sem((NOBJ,))],
    )

    (smoothed,) = local_call(
        smooth_kernel,
        "smooth",
        2,
        8,
        [(SMEM, rbf_support), (VMEM, sens.reshape(-1, LANES)), (VMEM, near(weights))],
        [(VMEM, shape((3 * NOBJ, NBLK * LANES), F32))],
        [pltpu.VMEM((n_row * NBLK * BPAD, LANES), F32)],
    )
    return (itout, resout, smoothed)


def solution(mesh):
    both = ("row", "col")
    in_specs = (
        P(None, both, None),
        P(None, both, None),
        P(None, both, None),
        P(None, None, both, None),
        P(None, None, both, None),
        P(),
        P(both, None, None, None),
        P(both, None),
        P(both, None),
        P(both, None),
        P(both),
        P(None, None, both),
        P(both, None),
        P(both, None, None, None),
    )
    out_specs = (P(None, both, None), P(None, both, None), P(None, both))
    return jax.shard_map(
        per_device, mesh=mesh, in_specs=in_specs, out_specs=out_specs, check_vma=False
    )
```

```python
import jax
import jax.numpy as jnp
import numpy as np
from jax import lax
from jax.experimental import pallas as pl
from jax.experimental.pallas import tpu as pltpu
from jax.sharding import PartitionSpec as P

NVAR = 5
NOBJ = 6
E = 96
H = 48
WMAX = 48
BLOCK = 320
TRACE = 80
LANES = 128
NBLK = 6
NSUP = 4
NBAS = 3
NVEC = NOBJ * NBAS
WIDE = NVEC * LANES
STEP = NBAS * LANES
SLOTS = 4 * H
FACES = 4 * E
VPAD = 24
WPAD = TRACE + 1
BPAD = 24
F32 = jnp.float32
BF16 = jnp.bfloat16


def selection():
    sel = np.zeros((BLOCK, 4 * LANES), np.float32)
    for var in range(NVAR):
        for a in range(4):
            for c in range(4):
                i = var * 16 + a * 4 + c
                base = var * 64
                sel[base + 48 + a * 4 + c, 0 * LANES + i] = 1
                sel[base + a * 4 + c, 1 * LANES + i] = 1
                sel[base + a * 16 + 12 + c, 2 * LANES + i] = 1
                sel[base + a * 16 + c, 3 * LANES + i] = 1
    return sel


def wall_spread():
    out = np.zeros((BLOCK, NVAR * LANES), np.float32)
    for var in range(NVAR):
        for p in range(16):
            out[var * 64 + p * 4, var * LANES + p : (var + 1) * LANES : 16] = 1
    return out


def dot(a, b, dims=((1,), (0,))):
    return lax.dot_general(a, b, (dims, ((), ())), preferred_element_type=F32)


def split(x):
    high = x.astype(BF16)
    return high, (x - high.astype(F32)).astype(BF16)


def picker(elements):
    n = elements.shape[1]
    row = lax.broadcasted_iota(jnp.int32, (E, n), 0)
    return jnp.where(row == elements, 1.0, 0.0).T.astype(BF16)


def fetch(pairs, sems):
    copies = [pltpu.make_async_copy(a, b, sems.at[n]) for n, (a, b) in enumerate(pairs)]
    for copy in copies:
        copy.start()
    return copies


def wait(*copies):
    for copy in copies:
        copy.wait()


def basis_kernel(
    flags, om_h, send_h, sel_h, r_h, d_h, s_h, sh_h, dots, table, us_h, o0, o1, o2, o3, om, send, sel, r, d, s, sh, us, sems, osems
):
    first = [(sel_h, sel), (sh_h, sh), (om_h, om), (send_h, send)]
    head = len(first)
    for k in range(NOBJ):
        first += [(r_h.at[k], r.at[k]), (d_h.at[:, k], d.at[:, k]), (s_h.at[:, k], s.at[:, k])]
    copies = fetch(first, sems)
    wait(*copies[:head])
    picks = [picker(send[f : f + 1, :]) for f in range(4)]
    stores = []
    for k in range(NOBJ):
        wait(*copies[head + 3 * k : head + 3 * k + 3])
        w = om[k]
        r0, d0, d1 = r[k], d[0, k], d[1, k]
        vecs = [w * r0, w * d0 + s[0, k], w * d1 + s[1, k]]
        for x, vec in enumerate([r0, d0, d1] + vecs):
            for i in range(2):
                dots[k, pl.ds(2 * x + i, 1), :] = jnp.sum(sh[i] * vec, axis=0, keepdims=True)
        dots[k, 12:16, :] = jnp.zeros((4, BLOCK), F32)
        for m, u in enumerate(vecs):
            us[k, m] = u
        stores += fetch([(us.at[k], us_h.at[k])], osems.at[k : k + 1])
        traces = dot(jnp.concatenate([u.astype(BF16) for u in vecs], axis=0), sel[...]).astype(BF16)
        at = slice(k * STEP, (k + 1) * STEP)
        for f, out in enumerate((o0, o1, o2, o3)):
            lanes = slice(f * LANES, (f + 1) * LANES)
            face = jnp.concatenate([traces[m * E : (m + 1) * E, lanes] for m in range(NBAS)], axis=1)
            table[f * H : (f + 1) * H, at] = face[H:]
            out[:, at] = dot(picks[f], face).astype(BF16)
    wait(*stores)


def relayout(b, f, wt, base, i, each=None):
    x = b[f, i].astype(F32)
    if each is not None:
        each(i, x)
    wt[pl.ds(base + i, E, stride=WPAD), 0:TRACE] = x.T


def blocks_kernel(_, perm_h, b_h, sh_h, selt_h, wt, q, hot, b, sh, selt, perm, qscr, square, sems):
    first = [(sh_h, sh), (selt_h, selt), (perm_h, perm)]
    copies = fetch(first + [(b_h.at[f], b.at[f]) for f in range(4)], sems)
    wait(*copies[:3])
    slot = perm[...]
    entry = jnp.where(slot < SLOTS, slot, SLOTS + (slot & 3) * H + (slot >> 2) - H)
    row = lax.broadcasted_iota(jnp.int32, (2 * SLOTS, FACES), 0)
    marks = jnp.where(row == entry, 1.0, 0.0).T
    for n in range(3):
        square[n] = marks[:, n * LANES : (n + 1) * LANES]
    parts = [split(sh[i]) for i in range(2)]
    nt = ((1,), (1,))
    for f in range(4):
        for n in range(3):
            lanes = slice(n * LANES, (n + 1) * LANES)
            hot[f * E : (f + 1) * E, lanes] = square[n, pl.ds(f, E, stride=4), :].astype(BF16)
        face = selt[f * LANES : (f + 1) * LANES, :]
        trsh = [(dot(face, high, nt) + dot(face, low, nt))[:TRACE] for high, low in parts]
        copies[3 + f].wait()

        def couple_shadow(i, x):
            for a in range(2):
                qscr[a, i * 8 : i * 8 + 8, 0:E] = jnp.sum((x * trsh[a]).reshape(TRACE // 8, 8, E), axis=0)

        for i in range(TRACE):
            relayout(b, f, wt, f * E * WPAD, i, couple_shadow)
        for a in range(2):
            total = sum(qscr[a, pl.ds(n, TRACE, stride=8), :] for n in range(8))
            q[a, f * E : (f + 1) * E, 0:TRACE] = total[:, 0:E].T
            q[a, f * E : (f + 1) * E, TRACE:LANES] = jnp.zeros((E, LANES - TRACE), F32)


def received(flags, recv, at):
    return [jnp.where(flags[d] > 0, ref[:, at], jnp.zeros((), BF16)) for d, ref in enumerate(recv)]


def merge_kernel(x, _, out):
    out[...] = jnp.broadcast_to(jnp.sum(x[...], axis=0, keepdims=True), out.shape)


def couple(t_ref, wt, base, y_ref, pad, face, e):
    at = pl.ds(face * pad, pad)
    block = wt[pl.ds(base + e * WPAD, TRACE), 0:TRACE].astype(BF16)
    y_ref[at, 0:TRACE] = dot(t_ref[at, 0:TRACE].astype(BF16), block)


def face_rows(y_ref, row, pad):
    return jnp.concatenate([y_ref[pl.ds(f * E * pad + row, E, stride=pad), :] for f in range(4)], axis=1)


def lifted(y, selt):
    high, low = split(y)
    both = dot(jnp.concatenate([high, low], axis=0), selt[...])
    return both[:E] + both[E:]


def apply_kernel(
    flags, hot, table, r0, r1, r2, r3, q, dots, wt, red, yn_h, rows, t_ref, y_ref, yn, osems
):
    y_ref[...] = jnp.zeros_like(y_ref)
    lane = lax.broadcasted_iota(jnp.int32, (16, LANES), 1)
    acc = jnp.zeros((16, LANES), F32)
    for k in range(NOBJ):
        at = slice(k * STEP, (k + 1) * STEP)
        full = jnp.concatenate(received(flags, (r0, r1, r2, r3), at) + [table[:, at]], axis=0)
        t = dot(hot[...], full)
        rows[k] = jnp.zeros((16, LANES), F32)
        for m in range(NBAS):
            part = t[:, m * LANES : (m + 1) * LANES]
            for f in range(4):
                to = pl.ds(f * E * VPAD + k * NBAS + m, E, stride=VPAD)
                t_ref[to, :] = part[f * E : (f + 1) * E]
            for i in range(2):
                rows[k, pl.ds(6 + 2 * m + i, 1), :] = jnp.sum(part * q[i], axis=0, keepdims=True)
        col = jnp.sum(rows[k], axis=1, keepdims=True) + jnp.sum(dots[k], axis=1, keepdims=True)
        acc += jnp.where(lane == k, col, 0.0)
    red[...] = jnp.broadcast_to(acc[None], red.shape)
    stores = []
    for f in range(4):
        for e in range(E):
            couple(t_ref, wt, f * E * WPAD, y_ref, VPAD, f * E + e, e)
        for k in range(NOBJ):
            for m in range(NBAS):
                yn[f, k, m] = y_ref[pl.ds(f * E * VPAD + k * NBAS + m, E, stride=VPAD), :]
        stores += fetch([(yn.at[f], yn_h.at[f])], osems.at[f : f + 1])
    wait(*stores)


def outgo_kernel(_, yn_h, send_h, cross_h, o0, o1, o2, o3, yn, send, cross, out, sems, osems):
    first = [(send_h, send), (cross_h, cross)] + [(yn_h.at[:, k], yn.at[:, k]) for k in range(NOBJ)]
    copies = fetch(first, sems)
    wait(*copies[:2])
    picks = [picker(send[f : f + 1, :]) for f in range(4)]
    for k in range(NOBJ):
        copies[2 + k].wait()
        ys = [jnp.concatenate([yn[f, k, m].astype(BF16) for f in range(4)], axis=1) for m in range(NBAS)]
        total = dot(jnp.concatenate(ys, axis=0), cross[...]).astype(BF16)
        at = slice(k * STEP, (k + 1) * STEP)
        for f in range(4):
            lanes = slice(f * LANES, (f + 1) * LANES)
            face = jnp.concatenate([total[m * E : (m + 1) * E, lanes] for m in range(NBAS)], axis=1)
            out[f, :, at] = dot(picks[f], face).astype(BF16)
    wait(*fetch([(out.at[f], o) for f, o in enumerate((o0, o1, o2, o3))], osems))


def solve(m00, m01, m10, m11, f0, f1):
    det = m00 * m11 - m01 * m10
    return (m11 * f0 - m01 * f1) / det, (m00 * f1 - m10 * f0) / det


def step_kernel(
    om, count, red, us_h, it_h, yn_h, wall, coef, selt_h, spread_h, itout_h, base_h, st2_h, coefs, payload, us, it, yn, selt, spread, itout, base, st2, points, scr, sems, osems
):
    first = [(selt_h, selt)]
    for k in range(NOBJ):
        first += [(us_h.at[k], us.at[k]), (yn_h.at[:, k], yn.at[:, k]), (it_h.at[k], it.at[k])]
    copies = fetch(first + [(spread_h, spread)], sems)
    t = jnp.sum(red[...], axis=0)
    row = lambda n: t[n : n + 1]
    lane = lax.broadcasted_iota(jnp.int32, (1, LANES), 1)
    w = sum(jnp.where(lane == k, om[k], 0.0) for k in range(NOBJ))
    c0, c1 = solve(row(2), row(4), row(3), row(5), row(0), row(1))
    n0 = -(row(6) - c0 * row(8) - c1 * row(10))
    n1 = -(row(7) - c0 * row(9) - c1 * row(11))
    e0, e1 = solve(n0, row(4), n1, row(5), row(0) + n0, row(1) + n1)
    gamma = w * (1.0 - e0)
    delta = gamma + e0
    for n, x in enumerate([c0, c1, 1.0 - delta, delta * c0, delta * c1 - e1, gamma, 1.0 / w, w]):
        coefs[pl.ds(n, 1), :] = x
    scr[...] = jnp.zeros_like(scr)
    slots = lax.broadcasted_iota(jnp.int32, (1, WMAX), 1)
    pick = picker(jnp.where(slots < count[0], wall[:, 0:WMAX], E))
    slot = lax.broadcasted_iota(jnp.int32, (WMAX, LANES), 0) % 8
    group = lax.broadcasted_iota(jnp.int32, (WMAX, LANES), 1) // 16
    mine = slot == group
    copies[0].wait()
    stores = []
    half = NOBJ * WMAX
    for k in range(NOBJ):
        wait(*copies[1 + 3 * k : 4 + 3 * k])
        c = [coefs[n : n + 1, k : k + 1] for n in range(7)]
        u0, u1, u2 = (us[k, m] for m in range(NBAS))
        st1 = u0 - c[0] * u1 - c[1] * u2
        y = [yn[f, k, 0] - c[0] * yn[f, k, 1] - c[1] * yn[f, k, 2] for f in range(4)]
        lift = lifted(jnp.concatenate(y, axis=1), selt)
        two = c[2] * u0 + c[3] * u1 + c[4] * u2 - c[5] * lift
        both = st1 + two
        new = it[k] + both
        itout[k] = new
        st2[k] = two[H:]
        base[k] = c[6] * u0 - both - lift
        outs = [(x.at[k], h.at[k]) for x, h in ((itout, itout_h), (st2, st2_h), (base, base_h))]
        stores += fetch(outs, osems.at[3 * k : 3 * k + 3])
        high, low = split(new)
        high, low = split(dot(pick, high) + dot(pick, low))
        points[k * WMAX : (k + 1) * WMAX, :] = high
        points[half + k * WMAX : half + (k + 1) * WMAX, :] = low
    copies[-1].wait()
    every = dot(points[...], spread[...])
    for k in range(NOBJ):
        at = slice(k * WMAX, (k + 1) * WMAX)
        below = slice(half + k * WMAX, half + (k + 1) * WMAX)
        wide = every[at] + every[below]
        sums = [None] * 3
        for var in range(NVAR):
            part = wide[:, var * LANES : (var + 1) * LANES]
            part = jnp.sum(jnp.where(mine, part, 0.0).reshape(NBLK, 8, LANES), axis=1)
            for a in range(3):
                term = coef[a * NVAR + var] * part
                sums[a] = term if sums[a] is None else sums[a] + term
        for a in range(3):
            scr[pl.ds(a * NOBJ + k, NBLK, stride=BPAD), :] = sums[a]
    payload[...] = jnp.broadcast_to(scr[...].astype(BF16)[None], payload.shape)
    wait(*stores)


def last_kernel(
    flags, coefs, hot, st2_h, base_h, a0, a1, a2, a3, b0_h, b1_h, b2_h, b3_h, blocks_h, sel_h, selt_h, w_h, _, out_h, weights, t_ref, y_ref, st2, base, b, blocks, w0, w1, w2, w3, sel, selt, out, sems, osems
):
    first = [(sel_h, sel), (st2_h, st2)] + [(h, b.at[d]) for d, h in enumerate((b0_h, b1_h, b2_h, b3_h))]
    first += [(blocks_h.at[f], blocks.at[f]) for f in range(4)] + [(selt_h, selt), (base_h, base), (w_h, weights)]
    copies = fetch(first, sems)
    y_ref[...] = jnp.zeros_like(y_ref)
    wait(*copies[:6])
    for k in range(NOBJ):
        c = [coefs[n : n + 1, k : k + 1] for n in range(6)]
        rows = []
        for d, a in enumerate((a0, a1, a2, a3)):
            u = [a[:, (k * NBAS + m) * LANES : (k * NBAS + m + 1) * LANES].astype(F32) for m in range(3)]
            y = [b[d, :, (k * NBAS + m) * LANES : (k * NBAS + m + 1) * LANES].astype(F32) for m in range(3)]
            x = c[2] * u[0] + c[3] * u[1] + c[4] * u[2] - c[5] * (y[0] - c[0] * y[1] - c[1] * y[2])
            rows.append(jnp.where(flags[d] > 0, x, 0.0).astype(BF16))
        local = dot(st2[k].astype(BF16), sel[...]).astype(BF16)
        rows += [local[:, f * LANES : (f + 1) * LANES] for f in range(4)]
        t = dot(hot[...], jnp.concatenate(rows, axis=0))
        for f in range(4):
            t_ref[pl.ds(f * E * 8 + k, E, stride=8), :] = t[f * E : (f + 1) * E]
    wts = (w0, w1, w2, w3)
    rounds = 16
    for f in range(5):
        if f < 4:
            copies[6 + f].wait()
        for n in range(rounds):
            for c in range(TRACE // rounds):
                if f < 4:
                    relayout(blocks, f, wts[f], 0, n * (TRACE // rounds) + c)
            for c in range(E // rounds):
                if f > 0:
                    e = n * (E // rounds) + c
                    couple(t_ref, wts[f - 1], 0, y_ref, 8, (f - 1) * E + e, e)
    wait(*copies[10:12])
    stores = []
    for k in range(NOBJ):
        out[k] = base[k] - lifted(face_rows(y_ref, k, 8), selt)
        stores += fetch([(out.at[k], out_h.at[k])], osems.at[k : k + 1])
    wait(*stores, *copies[12:])


def smooth_kernel(support, sens, weights, out, scr):
    scr[...] = sens[...].astype(F32)
    for m in range(NBLK):
        acc = None
        for s in range(NSUP):
            at = pl.multiple_of(support[m, s] * BPAD, 8)
            part = dot(scr[pl.ds(at, BPAD), :].astype(BF16), weights[m, s])
            acc = part if acc is None else acc + part
        out[:, m * LANES : (m + 1) * LANES] = acc[: 3 * NOBJ]


SMEM = pl.BlockSpec(memory_space=pltpu.SMEM)
ANY = pl.BlockSpec(memory_space=pl.ANY)
VMEM = pl.BlockSpec(memory_space=pltpu.VMEM)


def shape(dims, dtype):
    return jax.ShapeDtypeStruct(dims, dtype)


def far(x):
    return pltpu.with_memory_space_constraint(x, pltpu.HBM)


def near(x):
    return pltpu.with_memory_space_constraint(x, pltpu.VMEM)


def buffers(*arrays):
    return [pltpu.VMEM(x.shape, x.dtype) for x in arrays]


def local_call(kernel, name, us, mib, ins, outs, scratch):
    result = pl.pallas_call(
        kernel,
        in_specs=[spec for spec, _ in ins],
        out_specs=[spec for spec, _ in outs],
        out_shape=[x for _, x in outs],
        scratch_shapes=scratch,
        compiler_params=pltpu.CompilerParams(vmem_limit_bytes=mib << 20),
        cost_estimate=pl.CostEstimate(flops=int(us * 5e8), bytes_accessed=int(us * 1e6), transcendentals=0),
        name=name,
    )(*[x for _, x in ins])
    return result


def exchange(outgo):
    recv = []
    for d, (axis, shift) in enumerate((("row", 1), ("row", -1), ("col", 1), ("col", -1))):
        size = lax.axis_size(axis)
        recv.append(lax.ppermute(outgo[d], axis, [(i, (i + shift) % size) for i in range(size)]))
    return recv


def per_device(
    iterate,
    residual,
    shadow,
    res_dirs,
    sol_dirs,
    omega_step,
    face_blocks,
    send_list,
    neighbour_perm,
    wall_perm,
    wall_count,
    wall_coef,
    rbf_support,
    rbf_weights,
):
    n_row, n_col = lax.axis_size("row"), lax.axis_size("col")
    sel_np = selection()
    sel = jnp.asarray(sel_np, BF16)
    selt = jnp.asarray(sel_np.T, BF16)
    cross = jnp.asarray(sel_np.T @ sel_np, BF16)
    spread = jnp.asarray(wall_spread(), BF16)
    sem = pltpu.SemaphoreType.DMA
    fields = (NOBJ, E, BLOCK)
    traces = pltpu.VMEM((H, WIDE), BF16)

    spare = (4, NOBJ, NBAS, E, LANES)
    basis = (NOBJ, NBAS, E, BLOCK)

    row, col = lax.axis_index("row"), lax.axis_index("col")
    flags = jnp.stack([row > 0, row < n_row - 1, col > 0, col < n_col - 1]).astype(jnp.int32)
    dots, table, us, *outgo = local_call(
        basis_kernel,
        "basis",
        5,
        24,
        [(SMEM, flags)]
        + [(ANY, far(x)) for x in (omega_step, send_list, sel, residual, res_dirs, sol_dirs, shadow)],
        [
            (VMEM, pltpu.VMEM((NOBJ, 16, BLOCK), F32)),
            (VMEM, pltpu.VMEM((SLOTS, WIDE), BF16)),
            (ANY, pltpu.HBM(basis, F32)),
        ]
        + [(VMEM, traces)] * 4,
        [pltpu.SMEM((NOBJ,), F32)]
        + buffers(send_list, sel, residual, res_dirs, sol_dirs, shadow)
        + [pltpu.VMEM(basis, F32), sem((4 + 3 * NOBJ,)), sem((NOBJ,))],
    )
    recv = exchange(outgo)

    blocks = face_blocks.transpose(1, 2, 3, 0)
    wt, q, hot = local_call(
        blocks_kernel,
        "blocks",
        6,
        12,
        [(VMEM, near(dots))] + [(ANY, far(x)) for x in (neighbour_perm, blocks, shadow, selt)],
        [
            (VMEM, pltpu.VMEM((FACES * WPAD, LANES), F32)),
            (VMEM, pltpu.VMEM((2, FACES, LANES), F32)),
            (VMEM, pltpu.VMEM((FACES, 2 * SLOTS), BF16)),
        ],
        buffers(blocks, shadow, selt, neighbour_perm)
        + [pltpu.VMEM((2, TRACE * 8, LANES), F32), pltpu.VMEM((3, FACES, LANES), F32), sem((7,))],
    )

    red, yn = local_call(
        apply_kernel,
        "apply",
        7,
        24,
        [(SMEM, flags), (VMEM, near(hot)), (VMEM, near(table))]
        + [(VMEM, near(x)) for x in recv + [q, dots, wt]],
        [(VMEM, shape((n_row, 16, LANES), F32)), (ANY, pltpu.HBM(spare, F32))],
        [pltpu.VMEM((NOBJ, 16, LANES), F32)]
        + [pltpu.VMEM((FACES * VPAD, LANES), F32)] * 2
        + [pltpu.VMEM(spare, F32), sem((4,))],
    )
    outgo2 = local_call(
        outgo_kernel,
        "outgo",
        4,
        12,
        [(ANY, red)] + [(ANY, far(x)) for x in (yn, send_list, cross)],
        [(ANY, pltpu.HBM((H, WIDE), BF16))] * 4,
        [pltpu.VMEM(spare, F32)]
        + buffers(send_list, cross)
        + [pltpu.VMEM((4, H, WIDE), BF16), sem((2 + NOBJ,)), sem((4,))],
    )
    recv2 = exchange(outgo2)
    red_row = lax.all_to_all(red, "row", 0, 0, tiled=True)
    wall_coef, wall_perm, wall_count, rbf_support, red = lax.optimization_barrier(
        (wall_coef, wall_perm, wall_count, rbf_support, red)
    )
    coef = wall_coef.reshape(3 * NVAR, NBLK, LANES).astype(F32)
    (red_row,) = local_call(
        merge_kernel, "merge", 1, 4, [(VMEM, red_row), (ANY, far(outgo2[0]))], [(VMEM, shape((n_col, 16, LANES), F32))], []
    )
    red = lax.all_to_all(red_row, "col", 0, 0, tiled=True)

    payload = (n_row, NBLK * BPAD, LANES)
    upper = (NOBJ, E - H, BLOCK)
    itout, base, st2, coefs, payload = local_call(
        step_kernel,
        "step",
        6,
        32,
        [(SMEM, omega_step), (SMEM, wall_count), (VMEM, red)]
        + [(ANY, far(x)) for x in (us, iterate, yn)]
        + [(VMEM, wall_perm), (VMEM, near(coef)), (ANY, far(selt)), (ANY, far(spread))],
        [(ANY, shape(fields, F32)), (ANY, pltpu.HBM(fields, F32)), (ANY, pltpu.HBM(upper, F32))]
        + [(VMEM, pltpu.VMEM((8, LANES), F32)), (VMEM, shape(payload, BF16))],
        [pltpu.VMEM(basis, F32)]
        + buffers(iterate)
        + [pltpu.VMEM(spare, F32)]
        + buffers(selt, spread)
        + [pltpu.VMEM(fields, F32)] * 2
        + [pltpu.VMEM(upper, F32), pltpu.VMEM((2 * NOBJ * WMAX, BLOCK), BF16)]
        + [pltpu.VMEM((NBLK * BPAD, LANES), F32), sem((2 + 3 * NOBJ,)), sem((3 * NOBJ,))],
    )
    payload, *recv2 = lax.optimization_barrier((payload, *recv2))
    sens = lax.all_to_all(payload, "row", 0, 0, tiled=True)

    resout, weights = local_call(
        last_kernel,
        "last",
        8,
        40,
        [(SMEM, flags), (VMEM, near(coefs)), (VMEM, near(hot)), (ANY, far(st2)), (ANY, far(base))]
        + [(VMEM, near(x)) for x in recv]
        + [(ANY, far(x)) for x in recv2 + [blocks, sel, selt, rbf_weights]]
        + [(ANY, payload)],
        [(ANY, shape(fields, F32)), (VMEM, pltpu.VMEM(rbf_weights.shape, BF16))],
        [pltpu.VMEM((FACES * 8, LANES), F32)] * 2
        + [pltpu.VMEM(upper, F32), pltpu.VMEM(fields, F32), pltpu.VMEM((4, H, WIDE), BF16)]
        + buffers(blocks)
        + [pltpu.VMEM((E * WPAD, LANES), F32)] * 4
        + buffers(sel, selt, residual)
        + [sem((13,)), sem((NOBJ,))],
    )

    (smoothed,) = local_call(
        smooth_kernel,
        "smooth",
        2,
        8,
        [(SMEM, rbf_support), (VMEM, sens.reshape(-1, LANES)), (VMEM, near(weights))],
        [(VMEM, shape((3 * NOBJ, NBLK * LANES), F32))],
        [pltpu.VMEM((n_row * NBLK * BPAD, LANES), F32)],
    )
    return (itout, resout, smoothed)


def solution(mesh):
    both = ("row", "col")
    in_specs = (
        P(None, both, None),
        P(None, both, None),
        P(None, both, None),
        P(None, None, both, None),
        P(None, None, both, None),
        P(),
        P(both, None, None, None),
        P(both, None),
        P(both, None),
        P(both, None),
        P(both),
        P(None, None, both),
        P(both, None),
        P(both, None, None, None),
    )
    out_specs = (P(None, both, None), P(None, both, None), P(None, both))
    return jax.shard_map(
        per_device, mesh=mesh, in_specs=in_specs, out_specs=out_specs, check_vma=False
    )
```

```python
import jax
import jax.numpy as jnp
import numpy as np
from jax import lax
from jax.experimental import pallas as pl
from jax.experimental.pallas import tpu as pltpu
from jax.sharding import PartitionSpec as P

NVAR = 5
NOBJ = 6
E = 96
H = 48
WMAX = 48
BLOCK = 320
TRACE = 80
LANES = 128
NBLK = 6
NSUP = 4
NBAS = 3
NVEC = NOBJ * NBAS
WIDE = NVEC * LANES
STEP = NBAS * LANES
SLOTS = 4 * H
FACES = 4 * E
VPAD = 24
WPAD = TRACE + 1
BPAD = 24
F32 = jnp.float32
BF16 = jnp.bfloat16


def selection():
    sel = np.zeros((BLOCK, 4 * LANES), np.float32)
    for var in range(NVAR):
        for a in range(4):
            for c in range(4):
                i = var * 16 + a * 4 + c
                base = var * 64
                sel[base + 48 + a * 4 + c, 0 * LANES + i] = 1
                sel[base + a * 4 + c, 1 * LANES + i] = 1
                sel[base + a * 16 + 12 + c, 2 * LANES + i] = 1
                sel[base + a * 16 + c, 3 * LANES + i] = 1
    return sel


def wall_spread():
    out = np.zeros((BLOCK, NVAR * LANES), np.float32)
    for var in range(NVAR):
        for p in range(16):
            out[var * 64 + p * 4, var * LANES + p : (var + 1) * LANES : 16] = 1
    return out


def dot(a, b, dims=((1,), (0,))):
    return lax.dot_general(a, b, (dims, ((), ())), preferred_element_type=F32)


def split(x):
    high = x.astype(BF16)
    return high, (x - high.astype(F32)).astype(BF16)


def picker(elements):
    n = elements.shape[1]
    row = lax.broadcasted_iota(jnp.int32, (E, n), 0)
    return jnp.where(row == elements, 1.0, 0.0).T.astype(BF16)


def fetch(pairs, sems):
    copies = [pltpu.make_async_copy(a, b, sems.at[n]) for n, (a, b) in enumerate(pairs)]
    for copy in copies:
        copy.start()
    return copies


def wait(*copies):
    for copy in copies:
        copy.wait()


def basis_kernel(
    flags, om_h, send_h, sel_h, r_h, d_h, s_h, sh_h, dots, table, us_h, o0, o1, o2, o3, om, send, sel, r, d, s, sh, us, sems, osems
):
    first = [(sel_h, sel), (sh_h, sh), (om_h, om), (send_h, send)]
    head = len(first)
    for k in range(NOBJ):
        first += [(r_h.at[k], r.at[k]), (d_h.at[:, k], d.at[:, k]), (s_h.at[:, k], s.at[:, k])]
    copies = fetch(first, sems)
    wait(*copies[:head])
    picks = [picker(send[f : f + 1, :]) for f in range(4)]
    stores = []
    for k in range(NOBJ):
        wait(*copies[head + 3 * k : head + 3 * k + 3])
        w = om[k]
        r0, d0, d1 = r[k], d[0, k], d[1, k]
        vecs = [w * r0, w * d0 + s[0, k], w * d1 + s[1, k]]
        for x, vec in enumerate([r0, d0, d1] + vecs):
            for i in range(2):
                dots[k, pl.ds(2 * x + i, 1), :] = jnp.sum(sh[i] * vec, axis=0, keepdims=True)
        dots[k, 12:16, :] = jnp.zeros((4, BLOCK), F32)
        for m, u in enumerate(vecs):
            us[k, m] = u
        stores += fetch([(us.at[k], us_h.at[k])], osems.at[k : k + 1])
        traces = dot(jnp.concatenate([u.astype(BF16) for u in vecs], axis=0), sel[...]).astype(BF16)
        at = slice(k * STEP, (k + 1) * STEP)
        for f, out in enumerate((o0, o1, o2, o3)):
            lanes = slice(f * LANES, (f + 1) * LANES)
            face = jnp.concatenate([traces[m * E : (m + 1) * E, lanes] for m in range(NBAS)], axis=1)
            table[f * H : (f + 1) * H, at] = face[H:]
            out[:, at] = dot(picks[f], face).astype(BF16)
    wait(*stores)


def relayout(b, f, wt, base, i, each=None):
    x = b[f, i].astype(F32)
    if each is not None:
        each(i, x)
    wt[pl.ds(base + i, E, stride=WPAD), 0:TRACE] = x.T


def blocks_kernel(_, perm_h, b_h, sh_h, selt_h, wt, q, hot, b, sh, selt, perm, qscr, square, sems):
    first = [(sh_h, sh), (selt_h, selt), (perm_h, perm)]
    copies = fetch(first + [(b_h.at[f], b.at[f]) for f in range(4)], sems)
    wait(*copies[:3])
    slot = perm[...]
    entry = jnp.where(slot < SLOTS, slot, SLOTS + (slot & 3) * H + (slot >> 2) - H)
    row = lax.broadcasted_iota(jnp.int32, (2 * SLOTS, FACES), 0)
    marks = jnp.where(row == entry, 1.0, 0.0).T
    for n in range(3):
        square[n] = marks[:, n * LANES : (n + 1) * LANES]
    parts = [split(sh[i]) for i in range(2)]
    nt = ((1,), (1,))
    for f in range(4):
        for n in range(3):
            lanes = slice(n * LANES, (n + 1) * LANES)
            hot[f * E : (f + 1) * E, lanes] = square[n, pl.ds(f, E, stride=4), :].astype(BF16)
        face = selt[f * LANES : (f + 1) * LANES, :]
        trsh = [(dot(face, high, nt) + dot(face, low, nt))[:TRACE] for high, low in parts]
        copies[3 + f].wait()

        def couple_shadow(i, x):
            for a in range(2):
                qscr[a, i * 8 : i * 8 + 8, 0:E] = jnp.sum((x * trsh[a]).reshape(TRACE // 8, 8, E), axis=0)

        for i in range(TRACE):
            relayout(b, f, wt, f * E * WPAD, i, couple_shadow)
        for a in range(2):
            total = sum(qscr[a, pl.ds(n, TRACE, stride=8), :] for n in range(8))
            q[a, f * E : (f + 1) * E, 0:TRACE] = total[:, 0:E].T
            q[a, f * E : (f + 1) * E, TRACE:LANES] = jnp.zeros((E, LANES - TRACE), F32)


def received(flags, recv, at):
    return [jnp.where(flags[d] > 0, ref[:, at], jnp.zeros((), BF16)) for d, ref in enumerate(recv)]


def merge_kernel(x, _, out):
    out[...] = jnp.broadcast_to(jnp.sum(x[...], axis=0, keepdims=True), out.shape)


def couple(t_ref, wt, base, y_ref, pad, face, e):
    at = pl.ds(face * pad, pad)
    block = wt[pl.ds(base + e * WPAD, TRACE), 0:TRACE].astype(BF16)
    y_ref[at, 0:TRACE] = dot(t_ref[at, 0:TRACE].astype(BF16), block)


def face_rows(y_ref, row, pad):
    return jnp.concatenate([y_ref[pl.ds(f * E * pad + row, E, stride=pad), :] for f in range(4)], axis=1)


def lifted(y, selt):
    high, low = split(y)
    both = dot(jnp.concatenate([high, low], axis=0), selt[...])
    return both[:E] + both[E:]


def apply_kernel(
    flags, hot, table, r0, r1, r2, r3, q, dots, wt, red, yn_h, rows, t_ref, y_ref, yn, osems
):
    y_ref[...] = jnp.zeros_like(y_ref)
    lane = lax.broadcasted_iota(jnp.int32, (16, LANES), 1)
    acc = jnp.zeros((16, LANES), F32)
    for k in range(NOBJ):
        at = slice(k * STEP, (k + 1) * STEP)
        full = jnp.concatenate(received(flags, (r0, r1, r2, r3), at) + [table[:, at]], axis=0)
        t = dot(hot[...], full)
        rows[k] = jnp.zeros((16, LANES), F32)
        for m in range(NBAS):
            part = t[:, m * LANES : (m + 1) * LANES]
            for f in range(4):
                to = pl.ds(f * E * VPAD + k * NBAS + m, E, stride=VPAD)
                t_ref[to, :] = part[f * E : (f + 1) * E]
            for i in range(2):
                rows[k, pl.ds(6 + 2 * m + i, 1), :] = jnp.sum(part * q[i], axis=0, keepdims=True)
        col = jnp.sum(rows[k], axis=1, keepdims=True) + jnp.sum(dots[k], axis=1, keepdims=True)
        acc += jnp.where(lane == k, col, 0.0)
    red[...] = jnp.broadcast_to(acc[None], red.shape)
    stores = []
    for f in range(4):
        for e in range(E):
            couple(t_ref, wt, f * E * WPAD, y_ref, VPAD, f * E + e, e)
        for k in range(NOBJ):
            for m in range(NBAS):
                yn[f, k, m] = y_ref[pl.ds(f * E * VPAD + k * NBAS + m, E, stride=VPAD), :]
        stores += fetch([(yn.at[f], yn_h.at[f])], osems.at[f : f + 1])
    wait(*stores)


def outgo_kernel(_, yn_h, send_h, cross_h, o0, o1, o2, o3, yn, send, cross, out, sems, osems):
    first = [(send_h, send), (cross_h, cross)] + [(yn_h.at[:, k], yn.at[:, k]) for k in range(NOBJ)]
    copies = fetch(first, sems)
    wait(*copies[:2])
    picks = [picker(send[f : f + 1, :]) for f in range(4)]
    stores = []
    for k in range(NOBJ):
        copies[2 + k].wait()
        ys = [jnp.concatenate([yn[f, k, m].astype(BF16) for f in range(4)], axis=1) for m in range(NBAS)]
        total = dot(jnp.concatenate(ys, axis=0), cross[...]).astype(BF16)
        at = slice(k * STEP, (k + 1) * STEP)
        for f in range(4):
            lanes = slice(f * LANES, (f + 1) * LANES)
            face = jnp.concatenate([total[m * E : (m + 1) * E, lanes] for m in range(NBAS)], axis=1)
            out[f, :, at] = dot(picks[f], face).astype(BF16)
        outs = [(out.at[f, :, at], o.at[:, at]) for f, o in enumerate((o0, o1, o2, o3))]
        stores += fetch(outs, osems.at[4 * k : 4 * k + 4])
    wait(*stores)


def solve(m00, m01, m10, m11, f0, f1):
    det = m00 * m11 - m01 * m10
    return (m11 * f0 - m01 * f1) / det, (m00 * f1 - m10 * f0) / det


def step_kernel(
    om, count, red, us_h, it_h, yn_h, wall, coef, selt_h, spread_h, itout_h, base_h, st2_h, coefs, payload, us, it, yn, selt, spread, itout, base, st2, points, scr, sems, osems
):
    first = [(selt_h, selt)]
    for k in range(NOBJ):
        first += [(us_h.at[k], us.at[k]), (yn_h.at[:, k], yn.at[:, k]), (it_h.at[k], it.at[k])]
    copies = fetch(first + [(spread_h, spread)], sems)
    t = jnp.sum(red[...], axis=0)
    row = lambda n: t[n : n + 1]
    lane = lax.broadcasted_iota(jnp.int32, (1, LANES), 1)
    w = sum(jnp.where(lane == k, om[k], 0.0) for k in range(NOBJ))
    c0, c1 = solve(row(2), row(4), row(3), row(5), row(0), row(1))
    n0 = -(row(6) - c0 * row(8) - c1 * row(10))
    n1 = -(row(7) - c0 * row(9) - c1 * row(11))
    e0, e1 = solve(n0, row(4), n1, row(5), row(0) + n0, row(1) + n1)
    gamma = w * (1.0 - e0)
    delta = gamma + e0
    for n, x in enumerate([c0, c1, 1.0 - delta, delta * c0, delta * c1 - e1, gamma, 1.0 / w, w]):
        coefs[pl.ds(n, 1), :] = x
    scr[...] = jnp.zeros_like(scr)
    slots = lax.broadcasted_iota(jnp.int32, (1, WMAX), 1)
    pick = picker(jnp.where(slots < count[0], wall[:, 0:WMAX], E))
    slot = lax.broadcasted_iota(jnp.int32, (WMAX, LANES), 0) % 8
    group = lax.broadcasted_iota(jnp.int32, (WMAX, LANES), 1) // 16
    mine = slot == group
    copies[0].wait()
    stores = []
    half = NOBJ * WMAX
    for k in range(NOBJ):
        wait(*copies[1 + 3 * k : 4 + 3 * k])
        c = [coefs[n : n + 1, k : k + 1] for n in range(7)]
        u0, u1, u2 = (us[k, m] for m in range(NBAS))
        st1 = u0 - c[0] * u1 - c[1] * u2
        y = [yn[f, k, 0] - c[0] * yn[f, k, 1] - c[1] * yn[f, k, 2] for f in range(4)]
        lift = lifted(jnp.concatenate(y, axis=1), selt)
        two = c[2] * u0 + c[3] * u1 + c[4] * u2 - c[5] * lift
        both = st1 + two
        new = it[k] + both
        itout[k] = new
        st2[k] = two[H:]
        base[k] = c[6] * u0 - both - lift
        outs = [(x.at[k], h.at[k]) for x, h in ((itout, itout_h), (st2, st2_h), (base, base_h))]
        stores += fetch(outs, osems.at[3 * k : 3 * k + 3])
        high, low = split(new)
        high, low = split(dot(pick, high) + dot(pick, low))
        points[k * WMAX : (k + 1) * WMAX, :] = high
        points[half + k * WMAX : half + (k + 1) * WMAX, :] = low
    copies[-1].wait()
    every = dot(points[...], spread[...])
    for k in range(NOBJ):
        at = slice(k * WMAX, (k + 1) * WMAX)
        below = slice(half + k * WMAX, half + (k + 1) * WMAX)
        wide = every[at] + every[below]
        sums = [None] * 3
        for var in range(NVAR):
            part = wide[:, var * LANES : (var + 1) * LANES]
            part = jnp.sum(jnp.where(mine, part, 0.0).reshape(NBLK, 8, LANES), axis=1)
            for a in range(3):
                term = coef[a * NVAR + var] * part
                sums[a] = term if sums[a] is None else sums[a] + term
        for a in range(3):
            scr[pl.ds(a * NOBJ + k, NBLK, stride=BPAD), :] = sums[a]
    payload[...] = jnp.broadcast_to(scr[...].astype(BF16)[None], payload.shape)
    wait(*stores)


def last_kernel(
    flags, coefs, hot, st2_h, base_h, a0, a1, a2, a3, b0_h, b1_h, b2_h, b3_h, blocks_h, sel_h, selt_h, w_h, _, out_h, weights, t_ref, y_ref, st2, base, b, blocks, w0, w1, w2, w3, sel, selt, out, sems, osems
):
    first = [(sel_h, sel), (st2_h, st2)] + [(h, b.at[d]) for d, h in enumerate((b0_h, b1_h, b2_h, b3_h))]
    first += [(blocks_h.at[f], blocks.at[f]) for f in range(4)] + [(selt_h, selt), (base_h, base), (w_h, weights)]
    copies = fetch(first, sems)
    y_ref[...] = jnp.zeros_like(y_ref)
    wait(*copies[:6])
    for k in range(NOBJ):
        c = [coefs[n : n + 1, k : k + 1] for n in range(6)]
        rows = []
        for d, a in enumerate((a0, a1, a2, a3)):
            u = [a[:, (k * NBAS + m) * LANES : (k * NBAS + m + 1) * LANES].astype(F32) for m in range(3)]
            y = [b[d, :, (k * NBAS + m) * LANES : (k * NBAS + m + 1) * LANES].astype(F32) for m in range(3)]
            x = c[2] * u[0] + c[3] * u[1] + c[4] * u[2] - c[5] * (y[0] - c[0] * y[1] - c[1] * y[2])
            rows.append(jnp.where(flags[d] > 0, x, 0.0).astype(BF16))
        local = dot(st2[k].astype(BF16), sel[...]).astype(BF16)
        rows += [local[:, f * LANES : (f + 1) * LANES] for f in range(4)]
        t = dot(hot[...], jnp.concatenate(rows, axis=0))
        for f in range(4):
            t_ref[pl.ds(f * E * 8 + k, E, stride=8), :] = t[f * E : (f + 1) * E]
    wts = (w0, w1, w2, w3)
    rounds = 16
    for f in range(5):
        if f < 4:
            copies[6 + f].wait()
        for n in range(rounds):
            for c in range(TRACE // rounds):
                if f < 4:
                    relayout(blocks, f, wts[f], 0, n * (TRACE // rounds) + c)
            for c in range(E // rounds):
                if f > 0:
                    e = n * (E // rounds) + c
                    couple(t_ref, wts[f - 1], 0, y_ref, 8, (f - 1) * E + e, e)
    wait(*copies[10:12])
    stores = []
    for k in range(NOBJ):
        out[k] = base[k] - lifted(face_rows(y_ref, k, 8), selt)
        stores += fetch([(out.at[k], out_h.at[k])], osems.at[k : k + 1])
    wait(*stores, *copies[12:])


def smooth_kernel(support, sens, weights, out, scr):
    scr[...] = sens[...].astype(F32)
    for m in range(NBLK):
        acc = None
        for s in range(NSUP):
            at = pl.multiple_of(support[m, s] * BPAD, 8)
            part = dot(scr[pl.ds(at, BPAD), :].astype(BF16), weights[m, s])
            acc = part if acc is None else acc + part
        out[:, m * LANES : (m + 1) * LANES] = acc[: 3 * NOBJ]


SMEM = pl.BlockSpec(memory_space=pltpu.SMEM)
ANY = pl.BlockSpec(memory_space=pl.ANY)
VMEM = pl.BlockSpec(memory_space=pltpu.VMEM)


def shape(dims, dtype):
    return jax.ShapeDtypeStruct(dims, dtype)


def far(x):
    return pltpu.with_memory_space_constraint(x, pltpu.HBM)


def near(x):
    return pltpu.with_memory_space_constraint(x, pltpu.VMEM)


def buffers(*arrays):
    return [pltpu.VMEM(x.shape, x.dtype) for x in arrays]


def local_call(kernel, name, us, mib, ins, outs, scratch):
    result = pl.pallas_call(
        kernel,
        in_specs=[spec for spec, _ in ins],
        out_specs=[spec for spec, _ in outs],
        out_shape=[x for _, x in outs],
        scratch_shapes=scratch,
        compiler_params=pltpu.CompilerParams(vmem_limit_bytes=mib << 20),
        cost_estimate=pl.CostEstimate(flops=int(us * 5e8), bytes_accessed=int(us * 1e6), transcendentals=0),
        name=name,
    )(*[x for _, x in ins])
    return result


def exchange(outgo):
    recv = []
    for d, (axis, shift) in enumerate((("row", 1), ("row", -1), ("col", 1), ("col", -1))):
        size = lax.axis_size(axis)
        recv.append(lax.ppermute(outgo[d], axis, [(i, (i + shift) % size) for i in range(size)]))
    return recv


def per_device(
    iterate,
    residual,
    shadow,
    res_dirs,
    sol_dirs,
    omega_step,
    face_blocks,
    send_list,
    neighbour_perm,
    wall_perm,
    wall_count,
    wall_coef,
    rbf_support,
    rbf_weights,
):
    n_row, n_col = lax.axis_size("row"), lax.axis_size("col")
    sel_np = selection()
    sel = jnp.asarray(sel_np, BF16)
    selt = jnp.asarray(sel_np.T, BF16)
    cross = jnp.asarray(sel_np.T @ sel_np, BF16)
    spread = jnp.asarray(wall_spread(), BF16)
    sem = pltpu.SemaphoreType.DMA
    fields = (NOBJ, E, BLOCK)
    traces = pltpu.VMEM((H, WIDE), BF16)

    spare = (4, NOBJ, NBAS, E, LANES)
    basis = (NOBJ, NBAS, E, BLOCK)

    row, col = lax.axis_index("row"), lax.axis_index("col")
    flags = jnp.stack([row > 0, row < n_row - 1, col > 0, col < n_col - 1]).astype(jnp.int32)
    dots, table, us, *outgo = local_call(
        basis_kernel,
        "basis",
        5,
        24,
        [(SMEM, flags)]
        + [(ANY, far(x)) for x in (omega_step, send_list, sel, residual, res_dirs, sol_dirs, shadow)],
        [
            (VMEM, pltpu.VMEM((NOBJ, 16, BLOCK), F32)),
            (VMEM, pltpu.VMEM((SLOTS, WIDE), BF16)),
            (ANY, pltpu.HBM(basis, F32)),
        ]
        + [(VMEM, traces)] * 4,
        [pltpu.SMEM((NOBJ,), F32)]
        + buffers(send_list, sel, residual, res_dirs, sol_dirs, shadow)
        + [pltpu.VMEM(basis, F32), sem((4 + 3 * NOBJ,)), sem((NOBJ,))],
    )
    recv = exchange(outgo)

    blocks = face_blocks.transpose(1, 2, 3, 0)
    wt, q, hot = local_call(
        blocks_kernel,
        "blocks",
        6,
        12,
        [(VMEM, near(dots))] + [(ANY, far(x)) for x in (neighbour_perm, blocks, shadow, selt)],
        [
            (VMEM, pltpu.VMEM((FACES * WPAD, LANES), F32)),
            (VMEM, pltpu.VMEM((2, FACES, LANES), F32)),
            (VMEM, pltpu.VMEM((FACES, 2 * SLOTS), BF16)),
        ],
        buffers(blocks, shadow, selt, neighbour_perm)
        + [pltpu.VMEM((2, TRACE * 8, LANES), F32), pltpu.VMEM((3, FACES, LANES), F32), sem((7,))],
    )

    red, yn = local_call(
        apply_kernel,
        "apply",
        7,
        24,
        [(SMEM, flags), (VMEM, near(hot)), (VMEM, near(table))]
        + [(VMEM, near(x)) for x in recv + [q, dots, wt]],
        [(VMEM, shape((n_row, 16, LANES), F32)), (ANY, pltpu.HBM(spare, F32))],
        [pltpu.VMEM((NOBJ, 16, LANES), F32)]
        + [pltpu.VMEM((FACES * VPAD, LANES), F32)] * 2
        + [pltpu.VMEM(spare, F32), sem((4,))],
    )
    outgo2 = local_call(
        outgo_kernel,
        "outgo",
        4,
        12,
        [(ANY, red)] + [(ANY, far(x)) for x in (yn, send_list, cross)],
        [(ANY, pltpu.HBM((H, WIDE), BF16))] * 4,
        [pltpu.VMEM(spare, F32)]
        + buffers(send_list, cross)
        + [pltpu.VMEM((4, H, WIDE), BF16), sem((2 + NOBJ,)), sem((4 * NOBJ,))],
    )
    recv2 = exchange(outgo2)
    red_row = lax.all_to_all(red, "row", 0, 0, tiled=True)
    wall_coef, wall_perm, wall_count, rbf_support, red = lax.optimization_barrier(
        (wall_coef, wall_perm, wall_count, rbf_support, red)
    )
    coef = wall_coef.reshape(3 * NVAR, NBLK, LANES).astype(F32)
    (red_row,) = local_call(
        merge_kernel, "merge", 1, 4, [(VMEM, red_row), (ANY, far(outgo2[0]))], [(VMEM, shape((n_col, 16, LANES), F32))], []
    )
    red = lax.all_to_all(red_row, "col", 0, 0, tiled=True)

    payload = (n_row, NBLK * BPAD, LANES)
    upper = (NOBJ, E - H, BLOCK)
    itout, base, st2, coefs, payload = local_call(
        step_kernel,
        "step",
        6,
        32,
        [(SMEM, omega_step), (SMEM, wall_count), (VMEM, red)]
        + [(ANY, far(x)) for x in (us, iterate, yn)]
        + [(VMEM, wall_perm), (VMEM, near(coef)), (ANY, far(selt)), (ANY, far(spread))],
        [(ANY, shape(fields, F32)), (ANY, pltpu.HBM(fields, F32)), (ANY, pltpu.HBM(upper, F32))]
        + [(VMEM, pltpu.VMEM((8, LANES), F32)), (VMEM, shape(payload, BF16))],
        [pltpu.VMEM(basis, F32)]
        + buffers(iterate)
        + [pltpu.VMEM(spare, F32)]
        + buffers(selt, spread)
        + [pltpu.VMEM(fields, F32)] * 2
        + [pltpu.VMEM(upper, F32), pltpu.VMEM((2 * NOBJ * WMAX, BLOCK), BF16)]
        + [pltpu.VMEM((NBLK * BPAD, LANES), F32), sem((2 + 3 * NOBJ,)), sem((3 * NOBJ,))],
    )
    payload, *recv2 = lax.optimization_barrier((payload, *recv2))
    sens = lax.all_to_all(payload, "row", 0, 0, tiled=True)

    resout, weights = local_call(
        last_kernel,
        "last",
        8,
        40,
        [(SMEM, flags), (VMEM, near(coefs)), (VMEM, near(hot)), (ANY, far(st2)), (ANY, far(base))]
        + [(VMEM, near(x)) for x in recv]
        + [(ANY, far(x)) for x in recv2 + [blocks, sel, selt, rbf_weights]]
        + [(ANY, payload)],
        [(ANY, shape(fields, F32)), (VMEM, pltpu.VMEM(rbf_weights.shape, BF16))],
        [pltpu.VMEM((FACES * 8, LANES), F32)] * 2
        + [pltpu.VMEM(upper, F32), pltpu.VMEM(fields, F32), pltpu.VMEM((4, H, WIDE), BF16)]
        + buffers(blocks)
        + [pltpu.VMEM((E * WPAD, LANES), F32)] * 4
        + buffers(sel, selt, residual)
        + [sem((13,)), sem((NOBJ,))],
    )

    (smoothed,) = local_call(
        smooth_kernel,
        "smooth",
        2,
        8,
        [(SMEM, rbf_support), (VMEM, sens.reshape(-1, LANES)), (VMEM, near(weights))],
        [(VMEM, shape((3 * NOBJ, NBLK * LANES), F32))],
        [pltpu.VMEM((n_row * NBLK * BPAD, LANES), F32)],
    )
    return (itout, resout, smoothed)


def solution(mesh):
    both = ("row", "col")
    in_specs = (
        P(None, both, None),
        P(None, both, None),
        P(None, both, None),
        P(None, None, both, None),
        P(None, None, both, None),
        P(),
        P(both, None, None, None),
        P(both, None),
        P(both, None),
        P(both, None),
        P(both),
        P(None, None, both),
        P(both, None),
        P(both, None, None, None),
    )
    out_specs = (P(None, both, None), P(None, both, None), P(None, both))
    return jax.shard_map(
        per_device, mesh=mesh, in_specs=in_specs, out_specs=out_specs, check_vma=False
    )
```
